256 devices in a mesh: dp: 32 (over x, z), tensor: 8 (over y, core).
Axes of the slice: x: 4, y: 4, z: 8, core: 2. Of those that a mesh axis runs over, the one named last changes fastest.
Arguments:
- tokens_in: bfloat16 [4096, 8192], P('dp'), may hold values from -6 to 6
- out_grad: bfloat16 [4096, 8192], P('dp'), may hold values from -0.25 to 0.25
- up_grad: bfloat16 [4096, 28672], P('dp', 'tensor'), may hold values from -0.25 to 0.25
- hidden_act: bfloat16 [4096, 28672], P('dp', 'tensor'), may hold values from -6 to 6
- basis_up: bfloat16 [8192, 512], P('dp'), may hold values from -0.0625 to 0.0625
- basis_down: bfloat16 [8192, 512], P('dp'), may hold values from -0.0625 to 0.0625
- moment_up: float32 [512, 28672], P('dp', 'tensor'), may hold values from -4 to 4
- second_up: float32 [512, 28672], P('dp', 'tensor'), may hold values from 0.01 to 0.1
- moment_down: float32 [512, 28672], P('dp', 'tensor'), may hold values from -4 to 4
- second_down: float32 [512, 28672], P('dp', 'tensor'), may hold values from 0.01 to 0.1
Outputs:
- delta_up: bfloat16 [8192, 28672], P('dp', 'tensor')
- delta_down: bfloat16 [28672, 8192], P('tensor', 'dp')
- next_moment_up: float32 [512, 28672], P('dp', 'tensor')
- next_second_up: float32 [512, 28672], P('dp', 'tensor')
- next_moment_down: float32 [512, 28672], P('dp', 'tensor')
- next_second_down: float32 [512, 28672], P('dp', 'tensor')
The draws below stay inside these ranges and needn't reach their ends.
All inputs are finite; a program needn't handle non-finite values.
Results may differ from the reference program's by a relative error of at most 0.019.
Values may be sent and summed in bfloat16 or wider, within the bound.
A program may use at most 128 MiB of HBM per device.

```python
import math
import jax
import jax.numpy as jnp
from jax import lax

D = 8192
FF = 28672
R = 512
STEPS = 1000
TOK_DEV = 128
TOKENS = 4096
N_DP = 32


def levels(key, extent, shards, least, largest):
    level, own = 1.0, jax.random.fold_in(key, 6)
    for dim, parts in shards:
        draws = jnp.exp(jax.random.uniform(jax.random.fold_in(own, dim), (parts,), jnp.float32, least / len(shards), largest / len(shards)))
        level = level * jnp.repeat(draws, extent[dim] // parts).reshape([-1 if axis == dim else 1 for axis in range(len(extent))])
    return level


def gaussian(rng, extent, width, most, split=(), dtype=jnp.bfloat16):
    values = width * jax.random.normal(rng, extent, jnp.float32)
    if split:
        values = values * levels(rng, extent, split, -0.22, 0.18)
    return jnp.clip(values, -most, most).astype(dtype)


def setup_inputs(seed: int = 0) -> dict:
    key_of = jax.random.split(jax.random.key(seed), 11)
    tokens_in = gaussian(key_of[0], (TOKENS, D), 1.0, 6.0, ((0, 32),))
    out_grad = gaussian(key_of[1], (TOKENS, D), (TOKENS // 9) ** -0.5, 0.25, ((0, 32),))
    up_grad = gaussian(key_of[2], (TOKENS, FF), (TOKENS // 9) ** -0.5, 0.25, ((0, 32), (1, 8)))
    hidden_act = gaussian(key_of[3], (TOKENS, FF), 1.0, 6.0, ((0, 32), (1, 8)))
    basis_up = gaussian(key_of[4], (D, R), D ** -0.5, 0.0625, ((0, 32),))
    basis_down = gaussian(key_of[5], (D, R), D ** -0.5, 0.0625, ((0, 32),))
    moment_up = gaussian(key_of[6], (R, FF), 0.3, 4.0, ((0, 32), (1, 8)), jnp.float32)
    second_up = jnp.clip(jnp.exp(math.log(0.1) - 2.3025851 * jax.random.uniform(key_of[7], (R, FF), jnp.float32) ** levels(key_of[7], (R, FF), ((0, 32), (1, 8)), -0.2, 0.2)), 0.01, 0.1)
    moment_down = gaussian(key_of[8], (R, FF), 0.3, 4.0, ((0, 32), (1, 8)), jnp.float32)
    second_down = jnp.clip(jnp.exp(math.log(0.1) - 2.3025851 * jax.random.uniform(key_of[9], (R, FF), jnp.float32) ** levels(key_of[9], (R, FF), ((0, 32), (1, 8)), -0.2, 0.2)), 0.01, 0.1)
    return {"tokens_in": tokens_in, "out_grad": out_grad, "up_grad": up_grad, "hidden_act": hidden_act, "basis_up": basis_up, "basis_down": basis_down, "moment_up": moment_up, "second_up": second_up, "moment_down": moment_down, "second_down": second_down}


momentum_decay = 0.9
square_decay = 0.999
adam_epsilon = 1e-08
update_scale = 2.5

def block_sum(left, right):
    left_blocks = left.reshape(N_DP, TOK_DEV, left.shape[1])
    right_blocks = right.reshape(N_DP, TOK_DEV, right.shape[1])

    def accumulate(running, block_pair):
        product = jnp.dot(block_pair[0].T, block_pair[1], preferred_element_type=jnp.float32)
        rounded = lax.optimization_barrier(product.astype(jnp.bfloat16))
        return (running + rounded.astype(jnp.float32), None)
    start_sum = jnp.zeros((left.shape[1], right.shape[1]), jnp.float32)
    summed, unused = lax.scan(accumulate, start_sum, (left_blocks, right_blocks))
    return summed

def adam_update(gradient, moment, second):
    new_moment = momentum_decay * moment + (1.0 - momentum_decay) * gradient
    new_second = square_decay * second + (1.0 - square_decay) * gradient * gradient
    first_fix = 1.0 - momentum_decay ** STEPS
    second_fix = 1.0 - square_decay ** STEPS
    update = update_scale * (new_moment / first_fix) / (jnp.sqrt(new_second / second_fix) + adam_epsilon)
    return (new_moment, new_second, update.astype(jnp.bfloat16))

def reference(tokens_in, out_grad, up_grad, hidden_act, basis_up, basis_down, moment_up, second_up, moment_down, second_down):
    proj_tokens = jnp.dot(tokens_in, basis_up, preferred_element_type=jnp.float32).astype(jnp.bfloat16)
    proj_grads = jnp.dot(out_grad, basis_down, preferred_element_type=jnp.float32).astype(jnp.bfloat16)
    grad_up = block_sum(proj_tokens, up_grad)
    grad_down = block_sum(proj_grads, hidden_act)
    next_moment_up, next_second_up, step_up = adam_update(grad_up, moment_up, second_up)
    next_moment_down, next_second_down, step_down = adam_update(grad_down, moment_down, second_down)
    delta_up = jnp.dot(basis_up, step_up, preferred_element_type=jnp.float32).astype(jnp.bfloat16)
    delta_down = jnp.dot(step_down.T, basis_down.T, preferred_element_type=jnp.float32).astype(jnp.bfloat16)
    return (delta_up, delta_down, next_moment_up, next_second_up, next_moment_down, next_second_down)
```

```python
import functools

import jax
import jax.numpy as jnp
from jax import lax
from jax.experimental import pallas as pl
from jax.experimental.pallas import tpu as pltpu
from jax.sharding import PartitionSpec as P

STEPS = 1000
momentum_decay = 0.9
square_decay = 0.999
adam_epsilon = 1e-08
update_scale = 2.5
first_fix = 1.0 - momentum_decay**STEPS
second_fix = 1.0 - square_decay**STEPS

MESH = pl.DeviceIdType.MESH
BF, F32 = jnp.bfloat16, jnp.float32

NX, NY, NZ = 4, 4, 8
TOK, D, R, FD = 128, 8192, 512, 3584
BR = D // (NX * NZ)
RY = R // NY
Q = FD // NX
OWN = R // (NX * NZ)
ZROWS = NX * OWN
W1 = 2048
TILE = 512
N_SEM = 256


def kernel(
    tokens,
    out_grad,
    up_grad,
    hidden,
    basis_up,
    basis_down,
    m_up,
    v_up,
    m_down,
    v_down,
    delta_up,
    delta_down,
    grads_out,
    t_buf,
    b_all,
    b_own,
    acc,
    u_buf,
    relay,
    pt,
    g_buf,
    rs_out,
    rs_in,
    gx,
    gr,
    mom,
    steps,
    d_up,
    d_down,
    ssem,
    rsem,
    lsem,
):
    dp, tn = lax.axis_index("dp"), lax.axis_index("tensor")
    x, z = lax.div(dp, NZ), lax.rem(dp, NZ)
    y, c = lax.div(tn, 2), lax.rem(tn, 2)

    def wrap(v, n):
        return lax.rem(v + n, n)

    def at(xo=0, zo=0, yo=0, co=0):
        return (
            wrap(x + xo, NX) * NZ + wrap(z + zo, NZ),
            wrap(y + yo, NY) * 2 + lax.rem(c + co, 2),
        )

    def x_dev(xx):
        return (xx * NZ + z, tn)

    used = [0]
    pending = []

    def send(src, dst, dev):
        k = used[0]
        used[0] += 1
        cp = pltpu.make_async_remote_copy(
            src_ref=src,
            dst_ref=dst,
            send_sem=ssem.at[k],
            recv_sem=rsem.at[k],
            device_id=dev,
            device_id_type=MESH,
        )
        cp.start()
        pending.append(cp)
        return cp

    local_used = [0]

    def load(src, dst):
        k = local_used[0]
        local_used[0] += 1
        cp = pltpu.make_async_copy(src, dst, lsem.at[k])
        cp.start()
        return cp

    def load_by_core(src0, src1, dst):
        k = local_used[0]
        local_used[0] += 1

        @pl.when(c == 0)
        def _():
            pltpu.make_async_copy(src0, dst, lsem.at[k]).start()

        @pl.when(c == 1)
        def _():
            pltpu.make_async_copy(src1, dst, lsem.at[k]).start()

        return pltpu.make_async_copy(src0, dst, lsem.at[k])

    def quarter(q):
        return pl.ds(pl.multiple_of(q * Q, 128), Q)

    def tok_rows(q):
        return pl.ds(pl.multiple_of(q * TOK, TOK), TOK)

    y_cols = pl.ds(pl.multiple_of(y * RY, RY), RY)

    b_reg0 = b_all.at[x, z]
    own_b = load_by_core(basis_up.at[:, y_cols], basis_down.at[:, y_cols], b_reg0)
    own_t = load_by_core(tokens, out_grad, t_buf)
    ins = (up_grad, hidden)
    own_u = [load(ins[m].at[:, quarter(x)], u_buf.at[m, tok_rows(x), :]) for m in (0, 1)]
    own_m = [load(r, mom.at[k]) for k, r in enumerate((m_up, v_up, m_down, v_down))]
    own_bases = [load(r, b_own.at[k]) for k, r in enumerate((basis_up, basis_down))]

    partners = [at(xo=k) for k in range(1, NX)]
    partners += [at(zo=1), at(zo=-1)]
    partners += [at(yo=k) for k in range(1, NY)]
    partners += [at(co=1)]
    barrier = pltpu.get_barrier_semaphore()
    for dev in partners:
        pl.semaphore_signal(barrier, inc=1, device_id=dev, device_id_type=MESH)
    acc[...] = jnp.zeros_like(acc)
    own_b.wait()
    pl.semaphore_wait(barrier, len(partners))

    dirs = (1, -1)

    def b_reg(xo, zo, half=None):
        ref = b_all.at[wrap(x + xo, NX), wrap(z + zo, NZ)]
        if half is None:
            return ref
        return ref.at[pl.ds(half * (BR // 2), BR // 2), :]

    def gather_xz(reg):
        hx, hz = {}, {}

        def z_first(xb):
            for d in dirs:
                blk = reg(xb, 0)
                hz[xb, d, 1] = send(blk, blk, at(zo=d))

        def z_step(xb, k):
            for d in dirs:
                hz[xb, d, k].wait_recv()
                if k < 4:
                    half = None if k < 3 else (0 if d > 0 else 1)
                    blk = reg(xb, -d * k, half)
                    hz[xb, d, k + 1] = send(blk, blk, at(zo=d))
            return [(xb, k), (xb, -k)] if k < 4 else [(xb, 4)]

        def r0():
            for d in dirs:
                blk = reg(0, 0)
                hx[d, 1] = send(blk, blk, at(xo=d))
            z_first(0)
            return [(0, 0)]

        def r1():
            for d in dirs:
                hx[d, 1].wait_recv()
                blk = reg(-d, 0, 0 if d > 0 else 1)
                hx[d, 2] = send(blk, blk, at(xo=d))
            z_first(-1)
            z_first(1)
            return [(-1, 0), (1, 0)]

        def r2():
            done = z_step(0, 1)
            for d in dirs:
                hx[d, 2].wait_recv()
            z_first(2)
            return done + [(2, 0)]

        def later(pairs):
            def run():
                done = []
                for xb, k in pairs:
                    done += z_step(xb, k)
                return done

            return run

        return [
            r0,
            r1,
            r2,
            later([(0, 2), (-1, 1), (1, 1)]),
            later([(0, 3), (-1, 2), (1, 2), (2, 1)]),
            later([(0, 4), (-1, 3), (1, 3), (2, 2)]),
            later([(-1, 4), (1, 4), (2, 3)]),
            later([(2, 4)]),
        ]

    def project(blocks):
        for xo, zo in blocks:
            xx, zz = wrap(x + xo, NX), wrap(z + zo, NZ)
            cols = pl.ds(pl.multiple_of((xx * NZ + zz) * BR, BR), BR)
            acc[...] += jnp.dot(t_buf[:, cols], b_all[xx, zz], preferred_element_type=F32)

    x1 = x + 1 - 2 * lax.rem(x, 2)
    x3 = NX - 1 - x
    x2 = lax.rem(x + 2, NX)
    near = ((x1, x3), (x3, x1))
    hu = {}
    rounds = gather_xz(b_reg)
    blocks = rounds[0]()
    for m in (0, 1):
        p1, p2 = near[m]
        hu[m, "b"] = send(ins[m].at[:, quarter(x2)], relay.at[m], x_dev(p1))
    for m in (0, 1):
        p1, p2 = near[m]
        hu[m, "a"] = send(ins[m].at[:, quarter(p1)], u_buf.at[m, tok_rows(x), :], x_dev(p1))
    for m in (0, 1):
        p1, p2 = near[m]
        hu[m, "c"] = send(ins[m].at[:, quarter(p2)], u_buf.at[m, tok_rows(x), :], x_dev(p2))
    own_t.wait()
    project(blocks)
    for k in range(1, len(rounds)):
        blocks = rounds[k]()
        if k == 4:
            for m in (0, 1):
                p1, p2 = near[m]
                hu[m, "b"].wait_recv()
                hu[m, "d"] = send(relay.at[m], u_buf.at[m, tok_rows(p1), :], x_dev(p2))
        project(blocks)

    def p_reg(xo, half=None):
        rows = pl.ds(0, R) if half is None else pl.ds(half * (R // 2), R // 2)
        return pt.at[c, rows, tok_rows(wrap(x + xo, NX))]

    mine = pt.at[c, y_cols, tok_rows(x)]
    mine[...] = acc[...].T.astype(BF)
    hp = [send(mine, mine, at(yo=k)) for k in range(1, NY)]
    for cp in hp:
        cp.wait_recv()
    hx = {}
    for d in dirs:
        hx[d, 1] = send(p_reg(0), p_reg(0), at(xo=d))
    hc = [send(p_reg(0), p_reg(0), at(co=1))]
    for d in dirs:
        hx[d, 1].wait_recv()
        blk = p_reg(-d, 0 if d > 0 else 1)
        hx[d, 2] = send(blk, blk, at(xo=d))
        hc.append(send(p_reg(-d), p_reg(-d), at(co=1)))
    for d in dirs:
        hx[d, 2].wait_recv()
        blk = p_reg(2, 0 if d > 0 else 1)
        hc.append(send(blk, blk, at(co=1)))
    for m in (0, 1):
        own_u[m].wait()
        for k in ("a", "c", "d"):
            hu[m, k].wait_recv()
    for cp in hc:
        cp.wait_recv()

    def gradient(m):
        for k in range(NX):
            part = jnp.dot(pt[m, k * 128 : (k + 1) * 128, :], u_buf[m], preferred_element_type=F32)
            g_buf[m, :, k * OWN : (k + 1) * OWN, :] = part.reshape(NZ, OWN, Q)

    hr = {}
    reach = {(0, 1): 3, (0, -1): 4, (1, 1): 4, (1, -1): 3}

    def rs_step(m, s):
        for j, d in enumerate(dirs):
            n = reach[m, d]
            if s >= n:
                continue
            val = g_buf[m, wrap(z + d * (n - s), NZ)]
            if s:
                hr[m, d, s - 1].wait_recv()
                val = val + rs_in[m, j, s - 1].astype(F32)
            rs_out[m, j, s] = val.astype(BF)
            hr[m, d, s] = send(rs_out.at[m, j, s], rs_in.at[m, j, s], at(zo=d))

    for m in (0, 1):
        gradient(m)
        rs_step(m, 0)
    for s in range(1, 4):
        for m in (0, 1):
            rs_step(m, s)

    hg = {}
    for m in (0, 1):
        val = g_buf[m, z]
        for j, d in enumerate(dirs):
            n = reach[m, d]
            hr[m, d, n - 1].wait_recv()
            val = val + rs_in[m, j, n - 1].astype(F32)
        gx[m] = val.astype(BF).reshape(NX, OWN, Q)
        gr[m, :, quarter(x)] = gx[m, x]
        for k in range(1, NX):
            xx = wrap(x + k, NX)
            hg[m, k] = send(gx.at[m, xx], gr.at[m, :, quarter(x)], x_dev(xx))

    for cp in own_m:
        cp.wait()

    own_rows = pl.ds(pl.multiple_of(dp * OWN, OWN), OWN)

    def adam(m):
        for k in range(1, NX):
            hg[m, k].wait_recv()

        @pl.loop(0, FD // TILE)
        def _(t):
            cols = pl.ds(pl.multiple_of(t * TILE, TILE), TILE)
            grad = gr[m, :, cols].astype(F32)
            moment = momentum_decay * mom[2 * m, :, cols] + (1.0 - momentum_decay) * grad
            second = square_decay * mom[2 * m + 1, :, cols] + (1.0 - square_decay) * grad * grad
            step = (
                update_scale
                * (moment * (1.0 / first_fix))
                / (jnp.sqrt(second * (1.0 / second_fix)) + adam_epsilon)
            )
            steps[m, own_rows, cols] = step.astype(BF)

    def s_reg(m, lo, hi):
        def reg(xo, zo, half=None):
            rows = (wrap(x + xo, NX) * NZ + wrap(z + zo, NZ)) * OWN
            width = hi - lo
            start = lo
            if half is not None:
                width //= 2
                start += half * width
            return steps.at[m, pl.ds(pl.multiple_of(rows, OWN), OWN), pl.ds(start, width)]

        return reg

    def gather_zx(reg):
        hz, hx = {}, {}

        def x_first(zo):
            for d in dirs:
                blk = reg(0, zo)
                hx[zo, d, 1] = send(blk, blk, at(xo=d))

        def x_relay(zo):
            for d in dirs:
                hx[zo, d, 1].wait_recv()
                blk = reg(-d, zo, 0 if d > 0 else 1)
                hx[zo, d, 2] = send(blk, blk, at(xo=d))

        def z_step(k):
            for d in dirs:
                hz[d, k].wait_recv()
                if k < 4:
                    blk = reg(0, -d * k, None if k < 3 else (0 if d > 0 else 1))
                    hz[d, k + 1] = send(blk, blk, at(zo=d))
            if k < 4:
                x_first(-k)
                x_first(k)
            else:
                x_first(4)

        def r0():
            for d in dirs:
                blk = reg(0, 0)
                hz[d, 1] = send(blk, blk, at(zo=d))
            x_first(0)

        def r1():
            z_step(1)
            x_relay(0)

        def r2():
            z_step(2)
            x_relay(-1)
            x_relay(1)

        def r3():
            z_step(3)

        def r4():
            z_step(4)
            x_relay(-2)
            x_relay(2)

        def r5():
            x_relay(-3)
            x_relay(3)

        def r6():
            x_relay(4)

        def r7():
            for zo in (0, -1, 1, -2, 2, -3, 3, 4):
                for d in dirs:
                    hx[zo, d, 2].wait_recv()

        return [r0, r1, r2, r3, r4, r5, r6, r7]

    plans = []
    for m in (0, 1):
        a, b = gather_zx(s_reg(m, 0, W1)), gather_xz(s_reg(m, W1, FD))
        plans.append((a, b))

    def run_round(m, k):
        a, b = plans[m]
        if k < len(b):
            b[k]()
        if k < len(a):
            a[k]()

    out_cps = []

    def update_up():
        @pl.loop(0, FD // TILE)
        def _(t):
            cols = pl.ds(pl.multiple_of(t * TILE, TILE), TILE)
            d_up[:, cols] = jnp.dot(b_own[0], steps[0, :, cols], preferred_element_type=F32).astype(BF)

    def update_down():
        @pl.loop(0, FD // TILE)
        def _(t):
            cols = pl.ds(pl.multiple_of(t * TILE, TILE), TILE)
            val = jnp.dot(b_own[1], steps[1, :, cols], preferred_element_type=F32)
            d_down[cols, :] = val.T.astype(BF)

    adam(0)
    run_round(0, 0)
    adam(1)
    n_rounds = 8
    for k in range(n_rounds):
        if k + 1 < n_rounds:
            run_round(0, k + 1)
        if k + 1 == n_rounds - 1:
            out_cps.append(load(gr, grads_out))
            for cp in own_bases:
                cp.wait()
            run_round(1, k)
            update_up()
            out_cps.append(load(d_up, delta_up))
        else:
            run_round(1, k)
    update_down()
    out_cps.append(load(d_down, delta_down))
    for cp in out_cps:
        cp.wait()
    for cp in pending:
        cp.wait_send()
    assert used[0] <= N_SEM, used[0]


def local(
    tokens_in,
    out_grad,
    up_grad,
    hidden_act,
    basis_up,
    basis_down,
    moment_up,
    second_up,
    moment_down,
    second_down,
):
    hbm = pl.BlockSpec(memory_space=pl.ANY)
    vmem = pltpu.VMEM
    delta_up, delta_down, grads = pl.pallas_call(
        kernel,
        out_shape=(
            jax.ShapeDtypeStruct((BR, FD), BF),
            jax.ShapeDtypeStruct((FD, BR), BF),
            jax.ShapeDtypeStruct((2, OWN, FD), BF),
        ),
        in_specs=[hbm] * 10,
        out_specs=(hbm, hbm, hbm),
        scratch_shapes=[
            vmem((TOK, D), BF),
            vmem((NX, NZ, BR, RY), BF),
            vmem((2, BR, R), BF),
            vmem((TOK, RY), F32),
            vmem((2, NX * TOK, Q), BF),
            vmem((2, TOK, Q), BF),
            vmem((2, R, NX * TOK), BF),
            vmem((2, NZ, ZROWS, Q), F32),
            vmem((2, 2, 4, ZROWS, Q), BF),
            vmem((2, 2, 4, ZROWS, Q), BF),
            vmem((2, NX, OWN, Q), BF),
            vmem((2, OWN, FD), BF),
            vmem((4, OWN, FD), F32),
            vmem((2, R, FD), BF),
            vmem((BR, FD), BF),
            vmem((FD, BR), BF),
            pltpu.SemaphoreType.DMA((N_SEM,)),
            pltpu.SemaphoreType.DMA((N_SEM,)),
            pltpu.SemaphoreType.DMA((16,)),
        ],
        compiler_params=pltpu.CompilerParams(
            collective_id=0, has_side_effects=True, vmem_limit_bytes=56 * 1024 * 1024
        ),
    )(
        tokens_in,
        out_grad,
        up_grad,
        hidden_act,
        basis_up,
        basis_down,
        moment_up,
        second_up,
        moment_down,
        second_down,
    )
    grads = grads.astype(F32)

    def moments(grad, moment, second):
        return (
            momentum_decay * moment + (1.0 - momentum_decay) * grad,
            square_decay * second + (1.0 - square_decay) * grad * grad,
        )

    next_moment_up, next_second_up = moments(grads[0], moment_up, second_up)
    next_moment_down, next_second_down = moments(grads[1], moment_down, second_down)
    return (delta_up, delta_down, next_moment_up, next_second_up, next_moment_down, next_second_down)


def solution(mesh):
    row, both = P("dp", None), P("dp", "tensor")
    return jax.shard_map(
        local,
        mesh=mesh,
        in_specs=(row, row, both, both, row, row, both, both, both, both),
        out_specs=(both, P("tensor", "dp"), both, both, both, both),
        check_vma=False,
    )
```

```python
import functools

import jax
import jax.numpy as jnp
from jax import lax
from jax.experimental import pallas as pl
from jax.experimental.pallas import tpu as pltpu
from jax.sharding import PartitionSpec as P

STEPS = 1000
momentum_decay = 0.9
square_decay = 0.999
adam_epsilon = 1e-08
update_scale = 2.5
first_fix = 1.0 - momentum_decay**STEPS
second_fix = 1.0 - square_decay**STEPS

MESH = pl.DeviceIdType.MESH
BF, F32 = jnp.bfloat16, jnp.float32

NX, NY, NZ = 4, 4, 8
TOK, D, R, FD = 128, 8192, 512, 3584
BR = D // (NX * NZ)
RY = R // NY
Q = FD // NX
OWN = R // (NX * NZ)
ZROWS = NX * OWN
W1 = 2048
TILE = 512
N_SEM = 256


def kernel(
    tokens,
    out_grad,
    up_grad,
    hidden,
    basis_up,
    basis_down,
    m_up,
    v_up,
    m_down,
    v_down,
    d_up,
    steps_down,
    gr,
    t_buf,
    b_all,
    b_own,
    acc,
    u_buf,
    relay,
    pt,
    g_buf,
    rs_out,
    rs_in,
    gx,
    mom,
    steps_up,
    ssem,
    rsem,
    lsem,
):
    dp, tn = lax.axis_index("dp"), lax.axis_index("tensor")
    x, z = lax.div(dp, NZ), lax.rem(dp, NZ)
    y, c = lax.div(tn, 2), lax.rem(tn, 2)

    def wrap(v, n):
        return lax.rem(v + n, n)

    def at(xo=0, zo=0, yo=0, co=0):
        return (
            wrap(x + xo, NX) * NZ + wrap(z + zo, NZ),
            wrap(y + yo, NY) * 2 + lax.rem(c + co, 2),
        )

    def x_dev(xx):
        return (xx * NZ + z, tn)

    used = [0]
    pending = []

    def take(n):
        used[0] += n
        return used[0] - n

    def remote(src, dst, dev, k, rk):
        return pltpu.make_async_remote_copy(
            src_ref=src,
            dst_ref=dst,
            send_sem=ssem.at[k],
            recv_sem=rsem.at[rk],
            device_id=dev,
            device_id_type=MESH,
        )

    def send(src, dst, dev, k=None, rk=None):
        k = take(1) if k is None else k
        cp = remote(src, dst, dev, k, k if rk is None else rk)
        cp.start()
        pending.append(cp)
        return cp

    def landed(ref, rk):
        remote(ref, ref, at(co=1), 0, rk).wait_recv()

    local_used = [0]

    def load(src, dst):
        k = local_used[0]
        local_used[0] += 1
        cp = pltpu.make_async_copy(src, dst, lsem.at[k])
        cp.start()
        return cp

    def load_by_core(src0, src1, dst):
        k = local_used[0]
        local_used[0] += 1

        @pl.when(c == 0)
        def _():
            pltpu.make_async_copy(src0, dst, lsem.at[k]).start()

        @pl.when(c == 1)
        def _():
            pltpu.make_async_copy(src1, dst, lsem.at[k]).start()

        return pltpu.make_async_copy(src0, dst, lsem.at[k])

    def quarter(q):
        return pl.ds(pl.multiple_of(q * Q, 128), Q)

    def tok_rows(q):
        return pl.ds(pl.multiple_of(q * TOK, TOK), TOK)

    y_cols = pl.ds(pl.multiple_of(y * RY, RY), RY)

    b_reg0 = b_all.at[x, z]
    own_b = load_by_core(basis_up.at[:, y_cols], basis_down.at[:, y_cols], b_reg0)
    own_t = load_by_core(tokens, out_grad, t_buf)
    ins = (up_grad, hidden)
    own_u = load_by_core(
        up_grad.at[:, quarter(x)], hidden.at[:, quarter(x)], u_buf.at[c, tok_rows(x), :]
    )
    own_m = [load(r, mom.at[k]) for k, r in enumerate((m_up, v_up, m_down, v_down))]
    own_basis = load(basis_up, b_own)

    partners = [at(xo=i, yo=j) for i in range(NX) for j in range(NY) if i or j]
    partners += [at(xo=i, co=1) for i in range(NX)]
    partners += [at(zo=1), at(zo=-1)]
    barrier = pltpu.get_barrier_semaphore()
    for dev in partners:
        pl.semaphore_signal(barrier, inc=1, device_id=dev, device_id_type=MESH)
    acc[...] = jnp.zeros_like(acc)
    own_b.wait()
    pl.semaphore_wait(barrier, len(partners))

    dirs = (1, -1)

    def b_reg(xo, zo, half=None):
        ref = b_all.at[wrap(x + xo, NX), wrap(z + zo, NZ)]
        if half is None:
            return ref
        return ref.at[pl.ds(half * (BR // 2), BR // 2), :]

    def gather_xz(reg, direct):
        hx, hz = {}, {}

        def z_first(xb):
            for d in dirs:
                blk = reg(xb, 0)
                hz[xb, d, 1] = send(blk, blk, at(zo=d))

        def z_step(xb, k):
            for d in dirs:
                hz[xb, d, k].wait_recv()
                if k < 4:
                    half = None if k < 3 else (0 if d > 0 else 1)
                    blk = reg(xb, -d * k, half)
                    hz[xb, d, k + 1] = send(blk, blk, at(zo=d))
            return [(xb, k), (xb, -k)] if k < 4 else [(xb, 4)]

        def r0():
            blk = reg(0, 0)
            for d in dirs:
                hx[d, 1] = send(blk, blk, at(xo=d))
            if direct:
                hx[2] = send(blk, blk, at(xo=2))
            z_first(0)
            return [(0, 0)]

        def r1():
            for d in dirs:
                hx[d, 1].wait_recv()
                if not direct:
                    blk = reg(-d, 0, 0 if d > 0 else 1)
                    hx[d, 2] = send(blk, blk, at(xo=d))
            z_first(-1)
            z_first(1)
            return [(-1, 0), (1, 0)]

        def r2():
            done = z_step(0, 1)
            if direct:
                hx[2].wait_recv()
            else:
                for d in dirs:
                    hx[d, 2].wait_recv()
            z_first(2)
            return done + [(2, 0)]

        def later(pairs):
            def run():
                done = []
                for xb, k in pairs:
                    done += z_step(xb, k)
                return done

            return run

        if direct:
            return [
                r0,
                r1,
                r2,
                later([(-1, 1), (1, 1), (0, 2), (2, 1)]),
                later([(-1, 2), (1, 2), (0, 3), (2, 2)]),
                later([(-1, 3), (1, 3), (0, 4), (2, 3)]),
                later([(-1, 4), (1, 4), (2, 4)]),
            ]
        return [
            r0,
            r1,
            r2,
            later([(0, 2), (-1, 1), (1, 1)]),
            later([(0, 3), (-1, 2), (1, 2), (2, 1)]),
            later([(0, 4), (-1, 3), (1, 3), (2, 2)]),
            later([(-1, 4), (1, 4), (2, 3)]),
            later([(2, 4)]),
        ]

    def project(blocks):
        for xo, zo in blocks:
            xx, zz = wrap(x + xo, NX), wrap(z + zo, NZ)
            cols = pl.ds(pl.multiple_of((xx * NZ + zz) * BR, BR), BR)
            acc[...] += jnp.dot(t_buf[:, cols], b_all[xx, zz], preferred_element_type=F32)

    x1 = x + 1 - 2 * lax.rem(x, 2)
    x3 = NX - 1 - x
    x2 = lax.rem(x + 2, NX)
    near = ((x1, x3), (x3, x1))
    my_p1 = x1 + c * (x3 - x1)
    my_p2 = x3 + c * (x1 - x3)

    def core_dev(xx, m):
        return (xx * NZ + z, y * 2 + m)

    rounds = gather_xz(b_reg, True)
    blocks = rounds[0]()
    got_b, got_a, got_c = take(2), take(2), take(2)
    for m in (0, 1):
        p1, p2 = near[m]
        send(ins[m].at[:, quarter(x2)], relay.at[c], core_dev(p1, m), rk=got_b + c)
    for m in (0, 1):
        p1, p2 = near[m]
        send(ins[m].at[:, quarter(p1)], u_buf.at[c, tok_rows(x), :], core_dev(p1, m), rk=got_a + c)
    for m in (0, 1):
        p1, p2 = near[m]
        send(ins[m].at[:, quarter(p2)], u_buf.at[c, tok_rows(x), :], core_dev(p2, m), rk=got_c + c)
    k_own = take(1)
    own_there = [
        remote(ins[m].at[:, quarter(x)], u_buf.at[c, tok_rows(x), :], at(co=1), k_own, k_own)
        for m in (0, 1)
    ]

    @pl.when(c == 1)
    def _():
        own_there[0].start()

    @pl.when(c == 0)
    def _():
        own_there[1].start()

    pending.append(own_there[0])
    hd = []
    own_t.wait()
    project(blocks)
    for k in range(1, len(rounds)):
        blocks = rounds[k]()
        if k == 4:
            for h in (0, 1):
                landed(relay.at[h], got_b + h)
                hd.append(send(relay.at[h], u_buf.at[h, tok_rows(my_p1), :], x_dev(my_p2)))
        project(blocks)

    mine = pt.at[y_cols, tok_rows(x)]
    mine[...] = acc[...].T.astype(BF)
    hp = {}
    for xo in (0, 2, 1, -1):
        for yo in range(NY):
            if xo == 0 and yo == 0 or xo == 2 and yo > 1:
                continue
            hp[xo, yo] = send(mine, mine, at(xo=xo, yo=yo))
    hp[1, 0].wait_recv()
    hp[-1, 0].wait_recv()
    for yo in (2, 3):
        blk = pt.at[y_cols, tok_rows(wrap(x + 1, NX))]
        hp[2, yo] = send(blk, blk, at(xo=-1, yo=yo))
    own_u.wait()
    landed(u_buf.at[1 - c, tok_rows(x), :], k_own)
    for h in (0, 1):
        landed(u_buf.at[h, tok_rows(my_p1), :], got_a + h)
        landed(u_buf.at[h, tok_rows(my_p2), :], got_c + h)
    for cp in hd:
        cp.wait_recv()
    for key, cp in hp.items():
        if key not in ((1, 0), (-1, 0)):
            cp.wait_recv()

    def gradient(m):
        for k in range(NX):
            rows = pt[k * NZ * OWN : (k + 1) * NZ * OWN, :]
            part = jnp.dot(rows, u_buf[m], preferred_element_type=F32)
            g_buf[m, :, k * OWN : (k + 1) * OWN, :] = part.reshape(NZ, OWN, Q)

    hr = {}
    reach = {(0, 1): 3, (0, -1): 4, (1, 1): 4, (1, -1): 3}

    def rs_step(m, s):
        for j, d in enumerate(dirs):
            n = reach[m, d]
            if s >= n:
                continue
            val = g_buf[m, wrap(z + d * (n - s), NZ)]
            if s:
                hr[m, d, s - 1].wait_recv()
                val = val + rs_in[m, j, s - 1].astype(F32)
            rs_out[m, j, s] = val.astype(BF)
            hr[m, d, s] = send(rs_out.at[m, j, s], rs_in.at[m, j, s], at(zo=d))

    for m in (0, 1):
        gradient(m)
        rs_step(m, 0)
    for s in range(1, 4):
        for m in (0, 1):
            rs_step(m, s)

    got_g = [take(2) for _ in range(1, NX)]
    k_g = take(1)
    for h in (0, 1):
        val = g_buf[h, z]
        for j, d in enumerate(dirs):
            n = reach[h, d]
            hr[h, d, n - 1].wait_recv()
            val = val + rs_in[h, j, n - 1].astype(F32)
        gx[h] = val.astype(BF).reshape(NX, OWN, Q)
        for k in range(1, NX):
            xx = wrap(x + k, NX)
            send(gx.at[h, xx], gr.at[c, :, quarter(x)], core_dev(xx, h), rk=got_g[k - 1] + c)
    gr[c, :, quarter(x)] = gx[c, x]
    send(gx.at[1 - c, x], gr.at[c, :, quarter(x)], at(co=1), k=k_g)

    for cp in own_m:
        cp.wait()
    landed(gr.at[1 - c, :, quarter(x)], k_g)

    own_rows = pl.ds(pl.multiple_of(dp * OWN, OWN), OWN)
    steps = (steps_up, steps_down)

    def adam(m):
        for k in range(1, NX):
            landed(gr.at[m, :, quarter(wrap(x - k, NX))], got_g[k - 1] + m)

        @pl.loop(0, FD // TILE)
        def _(t):
            cols = pl.ds(pl.multiple_of(t * TILE, TILE), TILE)
            grad = gr[m, :, cols].astype(F32)
            moment = momentum_decay * mom[2 * m, :, cols] + (1.0 - momentum_decay) * grad
            second = square_decay * mom[2 * m + 1, :, cols] + (1.0 - square_decay) * grad * grad
            step = (
                update_scale
                * (moment * (1.0 / first_fix))
                / (jnp.sqrt(second * (1.0 / second_fix)) + adam_epsilon)
            )
            steps[m][own_rows, cols] = step.astype(BF)

    def s_reg(m, lo, hi):
        def reg(xo, zo, half=None):
            rows = (wrap(x + xo, NX) * NZ + wrap(z + zo, NZ)) * OWN
            width = hi - lo
            start = lo
            if half is not None:
                width //= 2
                start += half * width
            return steps[m].at[pl.ds(pl.multiple_of(rows, OWN), OWN), pl.ds(start, width)]

        return reg

    def gather_zx(reg):
        hz, hx = {}, {}

        def x_first(zo):
            for d in dirs:
                blk = reg(0, zo)
                hx[zo, d, 1] = send(blk, blk, at(xo=d))

        def x_relay(zo):
            for d in dirs:
                hx[zo, d, 1].wait_recv()
                blk = reg(-d, zo, 0 if d > 0 else 1)
                hx[zo, d, 2] = send(blk, blk, at(xo=d))

        def z_step(k):
            for d in dirs:
                hz[d, k].wait_recv()
                if k < 4:
                    blk = reg(0, -d * k, None if k < 3 else (0 if d > 0 else 1))
                    hz[d, k + 1] = send(blk, blk, at(zo=d))
            if k < 4:
                x_first(-k)
                x_first(k)
            else:
                x_first(4)

        def r0():
            for d in dirs:
                blk = reg(0, 0)
                hz[d, 1] = send(blk, blk, at(zo=d))
            x_first(0)

        def r1():
            z_step(1)
            x_relay(0)

        def r2():
            z_step(2)
            x_relay(-1)
            x_relay(1)

        def r3():
            z_step(3)

        def r4():
            z_step(4)
            x_relay(-2)
            x_relay(2)

        def r5():
            x_relay(-3)
            x_relay(3)

        def r6():
            x_relay(4)

        def r7():
            for zo in (0, -1, 1, -2, 2, -3, 3, 4):
                for d in dirs:
                    hx[zo, d, 2].wait_recv()

        return [r0, r1, r2, r3, r4, r5, r6, r7]

    plans = []
    for m in (0, 1):
        a, b = gather_zx(s_reg(m, 0, W1)), gather_xz(s_reg(m, W1, FD), False)
        plans.append((a, b))

    def run_round(m, k):
        a, b = plans[m]
        if k < len(b):
            b[k]()
        if k < len(a):
            a[k]()

    def update_up():
        @pl.loop(0, FD // TILE)
        def _(t):
            cols = pl.ds(pl.multiple_of(t * TILE, TILE), TILE)
            d_up[:, cols] = jnp.dot(b_own[...], steps_up[:, cols], preferred_element_type=F32).astype(BF)

    adam(0)
    run_round(0, 0)
    adam(1)
    n_rounds = 8
    for k in range(n_rounds):
        if k + 1 < n_rounds:
            run_round(0, k + 1)
        run_round(1, k)
        if k + 1 == n_rounds - 1:
            own_basis.wait()
            update_up()
    for cp in pending:
        cp.wait_send()
    assert used[0] <= N_SEM, used[0]


def finish(
    d_up,
    steps_down,
    gr,
    basis_down,
    m_up,
    v_up,
    m_down,
    v_down,
    delta_up,
    delta_down,
    next_m_up,
    next_v_up,
    next_m_down,
    next_v_down,
    d_down,
    new,
    sem,
):
    cps = []

    def store(src, dst):
        cp = pltpu.make_async_copy(src, dst, sem.at[len(cps)])
        cp.start()
        cps.append(cp)

    store(d_up, delta_up)
    old = ((m_up, v_up), (m_down, v_down))
    outs = ((next_m_up, next_v_up), (next_m_down, next_v_down))
    for k in (0, 1):
        grad = gr[k].astype(F32)
        new[k, 0] = momentum_decay * old[k][0][...] + (1.0 - momentum_decay) * grad
        new[k, 1] = square_decay * old[k][1][...] + (1.0 - square_decay) * grad * grad
        for j in (0, 1):
            store(new.at[k, j], outs[k][j])
    for t in range(FD // TILE):
        rows = pl.ds(t * TILE, TILE)
        val = jnp.dot(basis_down[...], steps_down[:, rows], preferred_element_type=F32)
        d_down[rows, :] = val.T.astype(BF)
        store(d_down.at[rows, :], delta_down.at[rows, :])
    for cp in cps:
        cp.wait()


def local(
    tokens_in,
    out_grad,
    up_grad,
    hidden_act,
    basis_up,
    basis_down,
    moment_up,
    second_up,
    moment_down,
    second_down,
):
    hbm = pl.BlockSpec(memory_space=pl.ANY)
    in_vmem = pl.BlockSpec(memory_space=pltpu.VMEM)
    vmem = pltpu.VMEM
    moments = (moment_up, second_up, moment_down, second_down)
    operands = (tokens_in, out_grad, up_grad, hidden_act, basis_up, basis_down, *moments)
    d_up, steps_down, grads = pl.pallas_call(
        kernel,
        out_shape=(vmem((BR, FD), BF), vmem((R, FD), BF), vmem((2, OWN, FD), BF)),
        in_specs=[hbm] * 10,
        out_specs=(in_vmem, in_vmem, in_vmem),
        scratch_shapes=[
            vmem((TOK, D), BF),
            vmem((NX, NZ, BR, RY), BF),
            vmem((BR, R), BF),
            vmem((TOK, RY), F32),
            vmem((2, NX * TOK, Q), BF),
            vmem((2, TOK, Q), BF),
            vmem((R, NX * TOK), BF),
            vmem((2, NZ, ZROWS, Q), F32),
            vmem((2, 2, 4, ZROWS, Q), BF),
            vmem((2, 2, 4, ZROWS, Q), BF),
            vmem((2, NX, OWN, Q), BF),
            vmem((4, OWN, FD), F32),
            vmem((R, FD), BF),
            pltpu.SemaphoreType.DMA((N_SEM,)),
            pltpu.SemaphoreType.DMA((N_SEM,)),
            pltpu.SemaphoreType.DMA((16,)),
        ],
        compiler_params=pltpu.CompilerParams(
            collective_id=0, has_side_effects=True, vmem_limit_bytes=36 * 1024 * 1024
        ),
    )(*(pltpu.with_memory_space_constraint(v, pltpu.HBM) for v in operands))
    small = jax.ShapeDtypeStruct((OWN, FD), F32)
    return pl.pallas_call(
        finish,
        out_shape=(
            jax.ShapeDtypeStruct((BR, FD), BF),
            jax.ShapeDtypeStruct((FD, BR), BF),
            small,
            small,
            small,
            small,
        ),
        in_specs=[in_vmem] * 8,
        out_specs=(hbm,) * 6,
        scratch_shapes=[
            vmem((FD, BR), BF),
            vmem((2, 2, OWN, FD), F32),
            pltpu.SemaphoreType.DMA((5 + FD // TILE,)),
        ],
        compiler_params=pltpu.CompilerParams(vmem_limit_bytes=16 * 1024 * 1024),
    )(d_up, steps_down, grads, basis_down, *moments)


def solution(mesh):
    row, both = P("dp", None), P("dp", "tensor")
    return jax.shard_map(
        local,
        mesh=mesh,
        in_specs=(row, row, both, both, row, row, both, both, both, both),
        out_specs=(both, P("tensor", "dp"), both, both, both, both),
        check_vma=False,
    )
```

```python
import functools

import jax
import jax.numpy as jnp
from jax import lax
from jax.experimental import pallas as pl
from jax.experimental.pallas import tpu as pltpu
from jax.sharding import PartitionSpec as P

STEPS = 1000
momentum_decay = 0.9
square_decay = 0.999
adam_epsilon = 1e-08
update_scale = 2.5
first_fix = 1.0 - momentum_decay**STEPS
second_fix = 1.0 - square_decay**STEPS

MESH = pl.DeviceIdType.MESH
BF, F32 = jnp.bfloat16, jnp.float32

NX, NY, NZ = 4, 4, 8
TOK, D, R, FD = 128, 8192, 512, 3584
BR = D // (NX * NZ)
RY = R // NY
Q = FD // NX
OWN = R // (NX * NZ)
ZROWS = NX * OWN
QS, QO = (512, 384), (0, 512)
FS = tuple(NX * w for w in QS)
W1 = (1280, 896)
TILE = 512
N_SEM = 320


def kernel(
    tokens,
    out_grad,
    up_grad,
    hidden,
    basis_up,
    basis_down,
    m_up,
    v_up,
    m_down,
    v_down,
    steps1,
    d_up,
    d_down,
    gr0,
    gr1,
    t_buf,
    b_all,
    b_own,
    acc,
    u_buf,
    relay,
    pt,
    g_buf,
    rs_out0,
    rs_out1,
    rs_in0,
    rs_in1,
    gx0,
    gx1,
    mom,
    steps0,
    ssem,
    rsem,
    lsem,
):
    dp, tn = lax.axis_index("dp"), lax.axis_index("tensor")
    x, z = lax.div(dp, NZ), lax.rem(dp, NZ)
    y, c = lax.div(tn, 2), lax.rem(tn, 2)

    def wrap(v, n):
        return lax.rem(v + n, n)

    def at(xo=0, zo=0, yo=0, co=0):
        return (
            wrap(x + xo, NX) * NZ + wrap(z + zo, NZ),
            wrap(y + yo, NY) * 2 + lax.rem(c + co, 2),
        )

    def x_dev(xx):
        return (xx * NZ + z, tn)

    used = [0]
    pending = []

    def take(n):
        used[0] += n
        return used[0] - n

    def remote(src, dst, dev, k, rk):
        return pltpu.make_async_remote_copy(
            src_ref=src,
            dst_ref=dst,
            send_sem=ssem.at[k],
            recv_sem=rsem.at[rk],
            device_id=dev,
            device_id_type=MESH,
        )

    def send(src, dst, dev, k=None, rk=None):
        k = take(1) if k is None else k
        cp = remote(src, dst, dev, k, k if rk is None else rk)
        cp.start()
        pending.append(cp)
        return cp

    def landed(ref, rk):
        remote(ref, ref, at(co=1), 0, rk).wait_recv()

    local_used = [0]

    def load(src, dst):
        k = local_used[0]
        local_used[0] += 1
        cp = pltpu.make_async_copy(src, dst, lsem.at[k])
        cp.start()
        return cp

    def load_by_core(src0, src1, dst):
        k = local_used[0]
        local_used[0] += 1

        @pl.when(c == 0)
        def _():
            pltpu.make_async_copy(src0, dst, lsem.at[k]).start()

        @pl.when(c == 1)
        def _():
            pltpu.make_async_copy(src1, dst, lsem.at[k]).start()

        return pltpu.make_async_copy(src0, dst, lsem.at[k])

    def quarter(q):
        return pl.ds(pl.multiple_of(q * Q, 128), Q)

    def tok_rows(q):
        return pl.ds(pl.multiple_of(q * TOK, TOK), TOK)

    y_cols = pl.ds(pl.multiple_of(y * RY, RY), RY)

    b_reg0 = b_all.at[x, z]
    own_b = load_by_core(basis_up.at[:, y_cols], basis_down.at[:, y_cols], b_reg0)
    own_t = load_by_core(tokens, out_grad, t_buf)
    ins = (up_grad, hidden)
    own_u = load_by_core(
        up_grad.at[:, quarter(x)], hidden.at[:, quarter(x)], u_buf.at[c, tok_rows(x), :]
    )
    own_bases = [load(r, b_own.at[k]) for k, r in enumerate((basis_up, basis_down))]
    own_m = [load(r, mom.at[k]) for k, r in enumerate((m_up, v_up, m_down, v_down))]

    partners = [at(xo=i, yo=j) for i in range(NX) for j in range(NY) if i or j]
    partners += [at(xo=i, co=1) for i in range(NX)]
    partners += [at(zo=1), at(zo=-1)]
    barrier = pltpu.get_barrier_semaphore()
    for dev in partners:
        pl.semaphore_signal(barrier, inc=1, device_id=dev, device_id_type=MESH)
    acc[...] = jnp.zeros_like(acc)
    own_b.wait()
    pl.semaphore_wait(barrier, len(partners))

    dirs = (1, -1)

    def b_reg(xo, zo, half=None):
        ref = b_all.at[wrap(x + xo, NX), wrap(z + zo, NZ)]
        if half is None:
            return ref
        return ref.at[pl.ds(half * (BR // 2), BR // 2), :]

    def gather_xz(reg, direct):
        hx, hz = {}, {}

        def z_first(xb):
            for d in dirs:
                blk = reg(xb, 0)
                hz[xb, d, 1] = send(blk, blk, at(zo=d))

        def z_step(xb, k):
            for d in dirs:
                hz[xb, d, k].wait_recv()
                if k < 4:
                    half = None if k < 3 else (0 if d > 0 else 1)
                    blk = reg(xb, -d * k, half)
                    hz[xb, d, k + 1] = send(blk, blk, at(zo=d))
            return [(xb, k), (xb, -k)] if k < 4 else [(xb, 4)]

        def r0():
            blk = reg(0, 0)
            for d in dirs:
                hx[d, 1] = send(blk, blk, at(xo=d))
            if direct:
                hx[2] = send(blk, blk, at(xo=2))
            z_first(0)
            return [(0, 0)]

        def r1():
            for d in dirs:
                hx[d, 1].wait_recv()
                if not direct:
                    blk = reg(-d, 0, 0 if d > 0 else 1)
                    hx[d, 2] = send(blk, blk, at(xo=d))
            z_first(-1)
            z_first(1)
            return [(-1, 0), (1, 0)]

        def r2():
            done = z_step(0, 1)
            if direct:
                hx[2].wait_recv()
            else:
                for d in dirs:
                    hx[d, 2].wait_recv()
            z_first(2)
            return done + [(2, 0)]

        def later(pairs):
            def run():
                done = []
                for xb, k in pairs:
                    done += z_step(xb, k)
                return done

            return run

        if direct:
            return [
                r0,
                r1,
                r2,
                later([(-1, 1), (1, 1), (0, 2), (2, 1)]),
                later([(-1, 2), (1, 2), (0, 3), (2, 2)]),
                later([(-1, 3), (1, 3), (0, 4), (2, 3)]),
                later([(-1, 4), (1, 4), (2, 4)]),
            ]
        return [
            r0,
            r1,
            r2,
            later([(0, 2), (-1, 1), (1, 1)]),
            later([(0, 3), (-1, 2), (1, 2), (2, 1)]),
            later([(0, 4), (-1, 3), (1, 3), (2, 2)]),
            later([(-1, 4), (1, 4), (2, 3)]),
            later([(2, 4)]),
        ]

    def project(blocks):
        for xo, zo in blocks:
            xx, zz = wrap(x + xo, NX), wrap(z + zo, NZ)
            cols = pl.ds(pl.multiple_of((xx * NZ + zz) * BR, BR), BR)
            acc[...] += jnp.dot(t_buf[:, cols], b_all[xx, zz], preferred_element_type=F32)

    x1 = x + 1 - 2 * lax.rem(x, 2)
    x3 = NX - 1 - x
    x2 = lax.rem(x + 2, NX)
    near = ((x1, x3), (x3, x1))
    my_p1 = x1 + c * (x3 - x1)
    my_p2 = x3 + c * (x1 - x3)

    def core_dev(xx, m):
        return (xx * NZ + z, y * 2 + m)

    rounds = gather_xz(b_reg, True)
    blocks = rounds[0]()
    got_b, got_a, got_c = take(2), take(2), take(2)
    for m in (0, 1):
        p1, p2 = near[m]
        send(ins[m].at[:, quarter(x2)], relay.at[c], core_dev(p1, m), rk=got_b + c)
    for m in (0, 1):
        p1, p2 = near[m]
        send(ins[m].at[:, quarter(p1)], u_buf.at[c, tok_rows(x), :], core_dev(p1, m), rk=got_a + c)
    for m in (0, 1):
        p1, p2 = near[m]
        send(ins[m].at[:, quarter(p2)], u_buf.at[c, tok_rows(x), :], core_dev(p2, m), rk=got_c + c)
    k_own = take(1)
    own_there = [
        remote(ins[m].at[:, quarter(x)], u_buf.at[c, tok_rows(x), :], at(co=1), k_own, k_own)
        for m in (0, 1)
    ]

    @pl.when(c == 1)
    def _():
        own_there[0].start()

    @pl.when(c == 0)
    def _():
        own_there[1].start()

    pending.append(own_there[0])
    hd = []
    own_t.wait()
    project(blocks)
    for k in range(1, len(rounds)):
        blocks = rounds[k]()
        if k == 4:
            for h in (0, 1):
                landed(relay.at[h], got_b + h)
                hd.append(send(relay.at[h], u_buf.at[h, tok_rows(my_p1), :], x_dev(my_p2)))
        project(blocks)

    mine = pt.at[y_cols, tok_rows(x)]
    mine[...] = acc[...].T.astype(BF)
    hp = {}
    for xo in (0, 2, 1, -1):
        for yo in range(NY):
            if xo == 0 and yo == 0 or xo == 2 and yo > 1:
                continue
            hp[xo, yo] = send(mine, mine, at(xo=xo, yo=yo))
    hp[1, 0].wait_recv()
    hp[-1, 0].wait_recv()
    for yo in (2, 3):
        blk = pt.at[y_cols, tok_rows(wrap(x + 1, NX))]
        hp[2, yo] = send(blk, blk, at(xo=-1, yo=yo))
    own_u.wait()
    landed(u_buf.at[1 - c, tok_rows(x), :], k_own)
    for h in (0, 1):
        landed(u_buf.at[h, tok_rows(my_p1), :], got_a + h)
        landed(u_buf.at[h, tok_rows(my_p2), :], got_c + h)
    for cp in hd:
        cp.wait_recv()
    for key, cp in hp.items():
        if key not in ((1, 0), (-1, 0)):
            cp.wait_recv()

    def cols_of(st):
        return pl.ds(QO[st], QS[st])

    def gradient(st, h):
        for k in range(NX):
            rows = pt[k * NZ * OWN : (k + 1) * NZ * OWN, :]
            part = jnp.dot(rows, u_buf[h, :, cols_of(st)], preferred_element_type=F32)
            g_buf[h, :, k * OWN : (k + 1) * OWN, cols_of(st)] = part.reshape(NZ, OWN, QS[st])

    rs_out, rs_in, gx, gr, steps = (rs_out0, rs_out1), (rs_in0, rs_in1), (gx0, gx1), (gr0, gr1), (steps0, steps1)
    hr = {}
    reach = {(0, 1): 3, (0, -1): 4, (1, 1): 4, (1, -1): 3}

    def rs_step(st, h, s):
        for j, d in enumerate(dirs):
            n = reach[h, d]
            if s >= n:
                continue
            val = g_buf[h, wrap(z + d * (n - s), NZ), :, cols_of(st)]
            if s:
                hr[st, h, d, s - 1].wait_recv()
                val = val + rs_in[st][h, j, s - 1].astype(F32)
            rs_out[st][h, j, s] = val.astype(BF)
            hr[st, h, d, s] = send(rs_out[st].at[h, j, s], rs_in[st].at[h, j, s], at(zo=d))

    got_g = [[take(2) for _ in range(1, NX)] for st in (0, 1)]
    k_g = [take(1) for st in (0, 1)]

    def place(st, q):
        return pl.ds(pl.multiple_of(q * QS[st], 128), QS[st])

    def to_owners(st):
        for h in (0, 1):
            val = g_buf[h, z, :, cols_of(st)]
            for j, d in enumerate(dirs):
                n = reach[h, d]
                hr[st, h, d, n - 1].wait_recv()
                val = val + rs_in[st][h, j, n - 1].astype(F32)
            gx[st][h] = val.astype(BF).reshape(NX, OWN, QS[st])
            for k in range(1, NX):
                xx = wrap(x + k, NX)
                dst = gr[st].at[c, :, place(st, x)]
                send(gx[st].at[h, xx], dst, core_dev(xx, h), rk=got_g[st][k - 1] + c)
        gr[st][c, :, place(st, x)] = gx[st][c, x]
        send(gx[st].at[1 - c, x], gr[st].at[c, :, place(st, x)], at(co=1), k=k_g[st])

    own_rows = pl.ds(pl.multiple_of(dp * OWN, OWN), OWN)

    def adam(st):
        landed(gr[st].at[1 - c, :, place(st, x)], k_g[st])
        for m in (0, 1):
            for k in range(1, NX):
                landed(gr[st].at[m, :, place(st, wrap(x - k, NX))], got_g[st][k - 1] + m)
            for q in range(NX):
                cols = pl.ds(q * Q + QO[st], QS[st])
                here = pl.ds(q * QS[st], QS[st])
                grad = gr[st][m, :, here].astype(F32)
                moment = momentum_decay * mom[2 * m, :, cols] + (1.0 - momentum_decay) * grad
                second = square_decay * mom[2 * m + 1, :, cols] + (1.0 - square_decay) * grad * grad
                step = (
                    update_scale
                    * (moment * (1.0 / first_fix))
                    / (jnp.sqrt(second * (1.0 / second_fix)) + adam_epsilon)
                )
                steps[st][m, own_rows, here] = step.astype(BF)

    def gather_zx(reg):
        hz, hx = {}, {}

        def x_first(zo):
            for d in dirs:
                blk = reg(0, zo)
                hx[zo, d, 1] = send(blk, blk, at(xo=d))

        def x_relay(zo):
            for d in dirs:
                hx[zo, d, 1].wait_recv()
                blk = reg(-d, zo, 0 if d > 0 else 1)
                hx[zo, d, 2] = send(blk, blk, at(xo=d))

        def z_step(k):
            for d in dirs:
                hz[d, k].wait_recv()
                if k < 4:
                    blk = reg(0, -d * k, None if k < 3 else (0 if d > 0 else 1))
                    hz[d, k + 1] = send(blk, blk, at(zo=d))
            if k < 4:
                x_first(-k)
                x_first(k)
            else:
                x_first(4)

        def r0():
            for d in dirs:
                blk = reg(0, 0)
                hz[d, 1] = send(blk, blk, at(zo=d))
            x_first(0)

        def r1():
            z_step(1)
            x_relay(0)

        def r2():
            z_step(2)
            x_relay(-1)
            x_relay(1)

        def r3():
            z_step(3)

        def r4():
            z_step(4)
            x_relay(-2)
            x_relay(2)

        def r5():
            x_relay(-3)
            x_relay(3)

        def r6():
            x_relay(4)

        def r7():
            for zo in (0, -1, 1, -2, 2, -3, 3, 4):
                for d in dirs:
                    hx[zo, d, 2].wait_recv()

        return [r0, r1, r2, r3, r4, r5, r6, r7]

    def s_reg(st, lo, hi):
        def reg(xo, zo, half=None):
            rows = (wrap(x + xo, NX) * NZ + wrap(z + zo, NZ)) * OWN
            rows = pl.ds(pl.multiple_of(rows, OWN), OWN)
            return steps[st].at[slice(None) if half is None else half, rows, lo:hi]

        return reg

    plans = [
        (gather_xz(s_reg(st, W1[st], FS[st]), False), gather_zx(s_reg(st, 0, W1[st])))
        for st in (0, 1)
    ]

    def run_round(st, k):
        for plan in plans[st]:
            plan[k]()

    def update():
        for t in range(FS[0] // TILE):
            cols = pl.ds(t * TILE, TILE)
            val = jnp.dot(b_own[0], steps0[0, :, cols], preferred_element_type=F32)
            d_up[:, cols] = val.astype(BF)
            val = jnp.dot(b_own[1], steps0[1, :, cols], preferred_element_type=F32)
            d_down[cols, :] = val.T.astype(BF)

    for st in (0, 1):
        for h in (0, 1):
            gradient(st, h)
            rs_step(st, h, 0)
    for k in range(1, 4):
        for st in (0, 1):
            for h in (0, 1):
                rs_step(st, h, k)
    to_owners(0)
    to_owners(1)
    for cp in own_m + own_bases:
        cp.wait()
    adam(0)
    run_round(0, 0)
    adam(1)
    run_round(1, 0)
    for k in range(1, 7):
        run_round(0, k)
        run_round(1, k)
    run_round(0, 7)
    update()
    run_round(1, 7)
    for cp in pending:
        cp.wait_send()
    assert used[0] <= N_SEM, used[0]


def finish(
    steps1,
    d_up0,
    d_down0,
    gr0,
    gr1,
    basis_up,
    basis_down,
    m_up,
    v_up,
    m_down,
    v_down,
    delta_up,
    delta_down,
    next_m_up,
    next_v_up,
    next_m_down,
    next_v_down,
    d_up,
    d_down,
    new,
    sem,
):
    cps = []

    def store(src, dst):
        cp = pltpu.make_async_copy(src, dst, sem.at[len(cps)])
        cp.start()
        cps.append(cp)

    def places(st, q):
        return pl.ds(q * QS[st], QS[st]), pl.ds(q * Q + QO[st], QS[st])

    for q in range(NX):
        here, there = places(0, q)
        store(d_up0.at[:, here], delta_up.at[:, there])
        store(d_down0.at[here, :], delta_down.at[there, :])
    old = ((m_up, v_up), (m_down, v_down))
    outs = ((next_m_up, next_v_up), (next_m_down, next_v_down))
    for k in (0, 1):
        for st, gr in enumerate((gr0, gr1)):
            for q in range(NX):
                here, there = places(st, q)
                grad = gr[k, :, here].astype(F32)
                moment, second = old[k][0][:, there], old[k][1][:, there]
                new[k, 0, :, there] = momentum_decay * moment + (1.0 - momentum_decay) * grad
                new[k, 1, :, there] = square_decay * second + (1.0 - square_decay) * grad * grad
        for j in (0, 1):
            store(new.at[k, j], outs[k][j])
    for q in range(NX):
        here, there = places(1, q)
        val = jnp.dot(basis_down[...], steps1[1, :, here], preferred_element_type=F32)
        d_down[here, :] = val.T.astype(BF)
        store(d_down.at[here, :], delta_down.at[there, :])
        val = jnp.dot(basis_up[...], steps1[0, :, here], preferred_element_type=F32)
        d_up[:, here] = val.astype(BF)
        store(d_up.at[:, here], delta_up.at[:, there])
    for cp in cps:
        cp.wait()


def local(
    tokens_in,
    out_grad,
    up_grad,
    hidden_act,
    basis_up,
    basis_down,
    moment_up,
    second_up,
    moment_down,
    second_down,
):
    hbm = pl.BlockSpec(memory_space=pl.ANY)
    in_vmem = pl.BlockSpec(memory_space=pltpu.VMEM)
    vmem = pltpu.VMEM
    moments = (moment_up, second_up, moment_down, second_down)
    operands = (tokens_in, out_grad, up_grad, hidden_act, basis_up, basis_down, *moments)
    kept = pl.pallas_call(
        kernel,
        out_shape=(
            vmem((2, R, FS[1]), BF),
            vmem((BR, FS[0]), BF),
            vmem((FS[0], BR), BF),
            vmem((2, OWN, FS[0]), BF),
            vmem((2, OWN, FS[1]), BF),
        ),
        in_specs=[hbm] * 10,
        out_specs=(in_vmem,) * 5,
        scratch_shapes=[
            vmem((TOK, D), BF),
            vmem((NX, NZ, BR, RY), BF),
            vmem((2, BR, R), BF),
            vmem((TOK, RY), F32),
            vmem((2, NX * TOK, Q), BF),
            vmem((2, TOK, Q), BF),
            vmem((R, NX * TOK), BF),
            vmem((2, NZ, ZROWS, Q), F32),
            vmem((2, 2, 4, ZROWS, QS[0]), BF),
            vmem((2, 2, 4, ZROWS, QS[1]), BF),
            vmem((2, 2, 4, ZROWS, QS[0]), BF),
            vmem((2, 2, 4, ZROWS, QS[1]), BF),
            vmem((2, NX, OWN, QS[0]), BF),
            vmem((2, NX, OWN, QS[1]), BF),
            vmem((4, OWN, FD), F32),
            vmem((2, R, FS[0]), BF),
            pltpu.SemaphoreType.DMA((N_SEM,)),
            pltpu.SemaphoreType.DMA((N_SEM,)),
            pltpu.SemaphoreType.DMA((16,)),
        ],
        compiler_params=pltpu.CompilerParams(
            collective_id=0, has_side_effects=True, vmem_limit_bytes=40 * 1024 * 1024
        ),
    )(*(pltpu.with_memory_space_constraint(v, pltpu.HBM) for v in operands))
    small = jax.ShapeDtypeStruct((OWN, FD), F32)
    return pl.pallas_call(
        finish,
        out_shape=(
            jax.ShapeDtypeStruct((BR, FD), BF),
            jax.ShapeDtypeStruct((FD, BR), BF),
            small,
            small,
            small,
            small,
        ),
        in_specs=[in_vmem] * 11,
        out_specs=(hbm,) * 6,
        scratch_shapes=[
            vmem((BR, FS[1]), BF),
            vmem((FS[1], BR), BF),
            vmem((2, 2, OWN, FD), F32),
            pltpu.SemaphoreType.DMA((4 + 4 * NX,)),
        ],
        compiler_params=pltpu.CompilerParams(vmem_limit_bytes=16 * 1024 * 1024),
    )(*kept, basis_up, basis_down, *moments)


def solution(mesh):
    row, both = P("dp", None), P("dp", "tensor")
    return jax.shard_map(
        local,
        mesh=mesh,
        in_specs=(row, row, both, both, row, row, both, both, both, both),
        out_specs=(both, P("tensor", "dp"), both, both, both, both),
        check_vma=False,
    )
```

```python
import functools

import jax
import jax.numpy as jnp
from jax import lax
from jax.experimental import pallas as pl
from jax.experimental.pallas import tpu as pltpu
from jax.sharding import PartitionSpec as P

STEPS = 1000
momentum_decay = 0.9
square_decay = 0.999
adam_epsilon = 1e-08
update_scale = 2.5
first_fix = 1.0 - momentum_decay**STEPS
second_fix = 1.0 - square_decay**STEPS

MESH = pl.DeviceIdType.MESH
BF, F32 = jnp.bfloat16, jnp.float32

NX, NY, NZ = 4, 4, 8
TOK, D, R, FD = 128, 8192, 512, 3584
BR = D // (NX * NZ)
RY = R // NY
Q = FD // NX
OWN = R // (NX * NZ)
ZROWS = NX * OWN
QS, QO = (512, 384), (0, 512)
FS = tuple(NX * w for w in QS)
DEPTH = 2
W1 = (1280, 896)
TILE = 512
N_SEM = 320


def kernel(
    tokens,
    out_grad,
    up_grad,
    hidden,
    basis_up,
    basis_down,
    m_up,
    v_up,
    m_down,
    v_down,
    steps1,
    d_up,
    d_down,
    gr0,
    gr1,
    t_buf,
    b_all,
    b_own,
    acc,
    u_buf,
    relay,
    pt,
    g_buf,
    rs_out0,
    rs_out1,
    rs_in0,
    rs_in1,
    gx0,
    gx1,
    mom,
    steps0,
    ssem,
    rsem,
    lsem,
):
    dp, tn = lax.axis_index("dp"), lax.axis_index("tensor")
    x, z = lax.div(dp, NZ), lax.rem(dp, NZ)
    y, c = lax.div(tn, 2), lax.rem(tn, 2)

    def wrap(v, n):
        return lax.rem(v + n, n)

    def at(xo=0, zo=0, yo=0, co=0):
        return (
            wrap(x + xo, NX) * NZ + wrap(z + zo, NZ),
            wrap(y + yo, NY) * 2 + lax.rem(c + co, 2),
        )

    def x_dev(xx):
        return (xx * NZ + z, tn)

    used = [0]
    pending = []
    slow = []
    done = [0]
    marks = []

    def drain():
        marks.append(len(pending))
        for cp in pending[done[0] : marks[-DEPTH]] if len(marks) >= DEPTH else ():
            cp.wait_send()
            done[0] += 1

    def take(n):
        used[0] += n
        return used[0] - n

    def remote(src, dst, dev, k, rk):
        return pltpu.make_async_remote_copy(
            src_ref=src,
            dst_ref=dst,
            send_sem=ssem.at[k],
            recv_sem=rsem.at[rk],
            device_id=dev,
            device_id_type=MESH,
        )

    def send(src, dst, dev, k=None, rk=None, sent=pending):
        k = take(1) if k is None else k
        cp = remote(src, dst, dev, k, k if rk is None else rk)
        cp.start()
        sent.append(cp)
        return cp

    def landed(ref, rk):
        remote(ref, ref, at(co=1), 0, rk).wait_recv()

    local_used = [0]

    def load(src, dst):
        k = local_used[0]
        local_used[0] += 1
        cp = pltpu.make_async_copy(src, dst, lsem.at[k])
        cp.start()
        return cp

    def load_by_core(src0, src1, dst):
        k = local_used[0]
        local_used[0] += 1

        @pl.when(c == 0)
        def _():
            pltpu.make_async_copy(src0, dst, lsem.at[k]).start()

        @pl.when(c == 1)
        def _():
            pltpu.make_async_copy(src1, dst, lsem.at[k]).start()

        return pltpu.make_async_copy(src0, dst, lsem.at[k])

    def quarter(q):
        return pl.ds(pl.multiple_of(q * Q, 128), Q)

    def tok_rows(q):
        return pl.ds(pl.multiple_of(q * TOK, TOK), TOK)

    y_cols = pl.ds(pl.multiple_of(y * RY, RY), RY)

    b_reg0 = b_all.at[z, 0]
    own_b = load_by_core(basis_up.at[:, y_cols], basis_down.at[:, y_cols], b_reg0)
    own_t = load_by_core(tokens, out_grad, t_buf)
    ins = (up_grad, hidden)
    own_u = load_by_core(
        up_grad.at[:, quarter(x)], hidden.at[:, quarter(x)], u_buf.at[c, tok_rows(x), :]
    )
    own_bases = [load(r, b_own.at[k]) for k, r in enumerate((basis_up, basis_down))]
    own_m = [load(r, mom.at[k]) for k, r in enumerate((m_up, v_up, m_down, v_down))]

    partners = [at(xo=i, yo=j) for i in range(NX) for j in range(NY) if i or j]
    partners += [at(xo=i, co=1) for i in range(NX)]
    partners += [at(zo=1), at(zo=-1)]
    barrier = pltpu.get_barrier_semaphore()
    for dev in partners:
        pl.semaphore_signal(barrier, inc=1, device_id=dev, device_id_type=MESH)
    acc[...] = jnp.zeros_like(acc)
    own_b.wait()
    pl.semaphore_wait(barrier, len(partners))

    dirs = (1, -1)

    OWN_X, SIDES, FAR = slice(0, 1), slice(1, 3), slice(3, 4)
    offset = (0, -1, 1, 2)

    def gather_basis():
        hx, hz = {}, {}

        def z_send(who, d, k, half=None):
            rows = slice(None) if half is None else pl.ds(half * (BR // 2), BR // 2)
            blk = b_all.at[wrap(z - d * (k - 1), NZ), who, rows, :]
            hz[who.start, d, k] = send(blk, blk, at(zo=d))

        def z_step(who, k):
            for d in dirs:
                hz[who.start, d, k].wait_recv()
                if k < 4:
                    z_send(who, d, k + 1, None if k < 3 else (0 if d > 0 else 1))
            slots = range(who.start, who.stop)
            return [(i, zo) for i in slots for zo in ((-k, k) if k < 4 else (4,))]

        def r0():
            for k, (i, xo) in enumerate(((1, 1), (2, -1), (3, 2))):
                hx[i] = send(b_all.at[z, 0], b_all.at[z, i], at(xo=xo))
            for d in dirs:
                z_send(OWN_X, d, 1)
            return [(0, 0)]

        def r1():
            hx[1].wait_recv()
            hx[2].wait_recv()
            for d in dirs:
                z_send(SIDES, d, 1)
            return [(1, 0), (2, 0)]

        def r2():
            got = z_step(OWN_X, 1)
            hx[3].wait_recv()
            for d in dirs:
                z_send(FAR, d, 1)
            return got + [(3, 0)]

        def later(pairs):
            def run():
                return [b for who, k in pairs for b in z_step(who, k)]

            return run

        return [
            r0,
            r1,
            r2,
            later([(SIDES, 1), (OWN_X, 2), (FAR, 1)]),
            later([(SIDES, 2), (OWN_X, 3), (FAR, 2)]),
            later([(SIDES, 3), (OWN_X, 4), (FAR, 3)]),
            later([(SIDES, 4), (FAR, 4)]),
        ]

    def gather_xz(reg):
        hx, hz = {}, {}

        def z_first(xb):
            for d in dirs:
                blk = reg(xb, 0)
                hz[xb, d, 1] = send(blk, blk, at(zo=d))

        def z_step(xb, k):
            for d in dirs:
                hz[xb, d, k].wait_recv()
                if k < 4:
                    half = None if k < 3 else (0 if d > 0 else 1)
                    blk = reg(xb, -d * k, half)
                    hz[xb, d, k + 1] = send(blk, blk, at(zo=d))
            return [(xb, k), (xb, -k)] if k < 4 else [(xb, 4)]

        def r0():
            blk = reg(0, 0)
            for d in dirs:
                hx[d, 1] = send(blk, blk, at(xo=d))
            z_first(0)
            return [(0, 0)]

        def r1():
            for d in dirs:
                hx[d, 1].wait_recv()
                blk = reg(-d, 0, 0 if d > 0 else 1)
                hx[d, 2] = send(blk, blk, at(xo=d))
            z_first(-1)
            z_first(1)
            return [(-1, 0), (1, 0)]

        def r2():
            done = z_step(0, 1)
            for d in dirs:
                hx[d, 2].wait_recv()
            z_first(2)
            return done + [(2, 0)]

        def later(pairs):
            def run():
                done = []
                for xb, k in pairs:
                    done += z_step(xb, k)
                return done

            return run

        return [
            r0,
            r1,
            r2,
            later([(0, 2), (-1, 1), (1, 1)]),
            later([(0, 3), (-1, 2), (1, 2), (2, 1)]),
            later([(0, 4), (-1, 3), (1, 3), (2, 2)]),
            later([(-1, 4), (1, 4), (2, 3)]),
            later([(2, 4)]),
        ]

    def project(blocks):
        for i, zo in blocks:
            xx, zz = wrap(x + offset[i], NX), wrap(z + zo, NZ)
            cols = pl.ds(pl.multiple_of((xx * NZ + zz) * BR, BR), BR)
            acc[...] += jnp.dot(t_buf[:, cols], b_all[zz, i], preferred_element_type=F32)

    x1 = x + 1 - 2 * lax.rem(x, 2)
    x3 = NX - 1 - x
    x2 = lax.rem(x + 2, NX)
    near = ((x1, x3), (x3, x1))
    my_p1 = x1 + c * (x3 - x1)
    my_p2 = x3 + c * (x1 - x3)

    def core_dev(xx, m):
        return (xx * NZ + z, y * 2 + m)

    rounds = gather_basis()
    blocks = rounds[0]()
    got_b, got_a, got_c = take(2), take(2), take(2)
    for m in (0, 1):
        p1, p2 = near[m]
        send(ins[m].at[:, quarter(x2)], relay.at[c], core_dev(p1, m), rk=got_b + c, sent=slow)
    for m in (0, 1):
        p1, p2 = near[m]
        send(ins[m].at[:, quarter(p1)], u_buf.at[c, tok_rows(x), :], core_dev(p1, m), rk=got_a + c, sent=slow)
    for m in (0, 1):
        p1, p2 = near[m]
        send(ins[m].at[:, quarter(p2)], u_buf.at[c, tok_rows(x), :], core_dev(p2, m), rk=got_c + c, sent=slow)
    k_own = take(1)
    own_there = [
        remote(ins[m].at[:, quarter(x)], u_buf.at[c, tok_rows(x), :], at(co=1), k_own, k_own)
        for m in (0, 1)
    ]

    @pl.when(c == 1)
    def _():
        own_there[0].start()

    @pl.when(c == 0)
    def _():
        own_there[1].start()

    slow.append(own_there[0])
    hd = []
    own_t.wait()
    project(blocks)
    for k in range(1, len(rounds)):
        blocks = rounds[k]()
        if k == 3:
            for h in (0, 1):
                landed(relay.at[h], got_b + h)
                hd.append(send(relay.at[h], u_buf.at[h, tok_rows(my_p1), :], x_dev(my_p2), sent=slow))
        project(blocks)
        drain()

    mine = pt.at[y_cols, tok_rows(x)]
    mine[...] = acc[...].T.astype(BF)
    hp = {}
    for xo in (2, 1, -1, 0):
        for yo in range(NY):
            if xo == 0 and yo == 0:
                continue
            hp[xo, yo] = send(mine, mine, at(xo=xo, yo=yo))
    own_u.wait()
    landed(u_buf.at[1 - c, tok_rows(x), :], k_own)
    for h in (0, 1):
        landed(u_buf.at[h, tok_rows(my_p1), :], got_a + h)
        landed(u_buf.at[h, tok_rows(my_p2), :], got_c + h)
    for cp in hd:
        cp.wait_recv()
    for key, cp in hp.items():
        cp.wait_recv()

    def cols_of(st):
        return pl.ds(QO[st], QS[st])

    def gradient(st, h):
        for k in range(NX):
            rows = pt[k * NZ * OWN : (k + 1) * NZ * OWN, :]
            part = jnp.dot(rows, u_buf[h, :, cols_of(st)], preferred_element_type=F32)
            g_buf[h, :, k * OWN : (k + 1) * OWN, cols_of(st)] = part.reshape(NZ, OWN, QS[st])

    rs_out, rs_in, gx, gr, steps = (rs_out0, rs_out1), (rs_in0, rs_in1), (gx0, gx1), (gr0, gr1), (steps0, steps1)
    hr = {}
    reach = {(0, 1): 3, (0, -1): 4, (1, 1): 4, (1, -1): 3}

    def rs_step(st, h, s):
        for j, d in enumerate(dirs):
            n = reach[h, d]
            if s >= n:
                continue
            val = g_buf[h, wrap(z + d * (n - s), NZ), :, cols_of(st)]
            if s:
                hr[st, h, d, s - 1].wait_recv()
                val = val + rs_in[st][h, j, s - 1].astype(F32)
            rs_out[st][h, j, s] = val.astype(BF)
            hr[st, h, d, s] = send(rs_out[st].at[h, j, s], rs_in[st].at[h, j, s], at(zo=d))

    got_g = [[take(2) for _ in range(1, NX)] for st in (0, 1)]
    k_g = [take(1) for st in (0, 1)]

    def place(st, q):
        return pl.ds(pl.multiple_of(q * QS[st], 128), QS[st])

    def to_owners(st):
        for h in (0, 1):
            val = g_buf[h, z, :, cols_of(st)]
            for j, d in enumerate(dirs):
                n = reach[h, d]
                hr[st, h, d, n - 1].wait_recv()
                val = val + rs_in[st][h, j, n - 1].astype(F32)
            gx[st][h] = val.astype(BF).reshape(NX, OWN, QS[st])
            for k in range(1, NX):
                xx = wrap(x + k, NX)
                dst = gr[st].at[c, :, place(st, x)]
                send(gx[st].at[h, xx], dst, core_dev(xx, h), rk=got_g[st][k - 1] + c)
        gr[st][c, :, place(st, x)] = gx[st][c, x]
        send(gx[st].at[1 - c, x], gr[st].at[c, :, place(st, x)], at(co=1), k=k_g[st])

    own_rows = pl.ds(pl.multiple_of(dp * OWN, OWN), OWN)

    def adam(st):
        landed(gr[st].at[1 - c, :, place(st, x)], k_g[st])
        for m in (0, 1):
            for k in range(1, NX):
                landed(gr[st].at[m, :, place(st, wrap(x - k, NX))], got_g[st][k - 1] + m)
            for q in range(NX):
                cols = pl.ds(q * Q + QO[st], QS[st])
                here = pl.ds(q * QS[st], QS[st])
                grad = gr[st][m, :, here].astype(F32)
                moment = momentum_decay * mom[2 * m, :, cols] + (1.0 - momentum_decay) * grad
                second = square_decay * mom[2 * m + 1, :, cols] + (1.0 - square_decay) * grad * grad
                step = (
                    update_scale
                    * (moment * (1.0 / first_fix))
                    / (jnp.sqrt(second * (1.0 / second_fix)) + adam_epsilon)
                )
                steps[st][m, own_rows, here] = step.astype(BF)

    def gather_zx(reg):
        hz, hx = {}, {}

        def x_first(zo):
            for d in dirs:
                blk = reg(0, zo)
                hx[zo, d, 1] = send(blk, blk, at(xo=d))

        def x_relay(zo):
            for d in dirs:
                hx[zo, d, 1].wait_recv()
                blk = reg(-d, zo, 0 if d > 0 else 1)
                hx[zo, d, 2] = send(blk, blk, at(xo=d))

        def z_step(k):
            for d in dirs:
                hz[d, k].wait_recv()
                if k < 4:
                    blk = reg(0, -d * k, None if k < 3 else (0 if d > 0 else 1))
                    hz[d, k + 1] = send(blk, blk, at(zo=d))
            if k < 4:
                x_first(-k)
                x_first(k)
            else:
                x_first(4)

        def r0():
            for d in dirs:
                blk = reg(0, 0)
                hz[d, 1] = send(blk, blk, at(zo=d))
            x_first(0)

        def r1():
            z_step(1)
            x_relay(0)

        def r2():
            z_step(2)
            x_relay(-1)
            x_relay(1)

        def r3():
            z_step(3)

        def r4():
            z_step(4)
            x_relay(-2)
            x_relay(2)

        def r5():
            x_relay(-3)
            x_relay(3)

        def r6():
            x_relay(4)

        def r7():
            for zo in (0, -1, 1, -2, 2, -3, 3, 4):
                for d in dirs:
                    hx[zo, d, 2].wait_recv()

        return [r0, r1, r2, r3, r4, r5, r6, r7]

    def s_reg(st, lo, hi):
        def reg(xo, zo, half=None):
            rows = (wrap(x + xo, NX) * NZ + wrap(z + zo, NZ)) * OWN
            rows = pl.ds(pl.multiple_of(rows, OWN), OWN)
            return steps[st].at[slice(None) if half is None else half, rows, lo:hi]

        return reg

    plans = [
        (gather_xz(s_reg(st, W1[st], FS[st])), gather_zx(s_reg(st, 0, W1[st])))
        for st in (0, 1)
    ]

    def run_round(st, k):
        for plan in plans[st]:
            plan[k]()

    def update():
        for t in range(FS[0] // TILE):
            cols = pl.ds(t * TILE, TILE)
            val = jnp.dot(b_own[0], steps0[0, :, cols], preferred_element_type=F32)
            d_up[:, cols] = val.astype(BF)
            val = jnp.dot(b_own[1], steps0[1, :, cols], preferred_element_type=F32)
            d_down[cols, :] = val.T.astype(BF)

    for st in (0, 1):
        for h in (0, 1):
            gradient(st, h)
            rs_step(st, h, 0)
    for cp in slow:
        cp.wait_send()
    for k in range(1, 4):
        drain()
        for st in (0, 1):
            for h in (0, 1):
                rs_step(st, h, k)
    to_owners(0)
    to_owners(1)
    for cp in own_m + own_bases:
        cp.wait()
    adam(0)
    run_round(0, 0)
    adam(1)
    run_round(1, 0)
    for k in range(1, 7):
        run_round(0, k)
        run_round(1, k)
        drain()
    run_round(0, 7)
    update()
    run_round(1, 7)
    for cp in pending[done[0] :]:
        cp.wait_send()
    assert used[0] <= N_SEM, used[0]


def finish(
    steps1,
    d_up0,
    d_down0,
    gr0,
    gr1,
    basis_up,
    basis_down,
    m_up,
    v_up,
    m_down,
    v_down,
    delta_up,
    delta_down,
    next_m_up,
    next_v_up,
    next_m_down,
    next_v_down,
    d_up,
    d_down,
    new,
    sem,
):
    cps = []

    def store(src, dst):
        cp = pltpu.make_async_copy(src, dst, sem.at[len(cps)])
        cp.start()
        cps.append(cp)

    def places(st, q):
        return pl.ds(q * QS[st], QS[st]), pl.ds(q * Q + QO[st], QS[st])

    for q in range(NX):
        here, there = places(0, q)
        store(d_up0.at[:, here], delta_up.at[:, there])
        store(d_down0.at[here, :], delta_down.at[there, :])
    old = ((m_up, v_up), (m_down, v_down))
    outs = ((next_m_up, next_v_up), (next_m_down, next_v_down))
    for k in (0, 1):
        for st, gr in enumerate((gr0, gr1)):
            for q in range(NX):
                here, there = places(st, q)
                grad = gr[k, :, here].astype(F32)
                moment, second = old[k][0][:, there], old[k][1][:, there]
                new[k, 0, :, there] = momentum_decay * moment + (1.0 - momentum_decay) * grad
                new[k, 1, :, there] = square_decay * second + (1.0 - square_decay) * grad * grad
        for j in (0, 1):
            store(new.at[k, j], outs[k][j])
    for q in range(NX):
        here, there = places(1, q)
        val = jnp.dot(basis_down[...], steps1[1, :, here], preferred_element_type=F32)
        d_down[here, :] = val.T.astype(BF)
        store(d_down.at[here, :], delta_down.at[there, :])
        val = jnp.dot(basis_up[...], steps1[0, :, here], preferred_element_type=F32)
        d_up[:, here] = val.astype(BF)
        store(d_up.at[:, here], delta_up.at[:, there])
    for cp in cps:
        cp.wait()


def local(
    tokens_in,
    out_grad,
    up_grad,
    hidden_act,
    basis_up,
    basis_down,
    moment_up,
    second_up,
    moment_down,
    second_down,
):
    hbm = pl.BlockSpec(memory_space=pl.ANY)
    in_vmem = pl.BlockSpec(memory_space=pltpu.VMEM)
    vmem = pltpu.VMEM
    moments = (moment_up, second_up, moment_down, second_down)
    operands = (tokens_in, out_grad, up_grad, hidden_act, basis_up, basis_down, *moments)
    kept = pl.pallas_call(
        kernel,
        out_shape=(
            vmem((2, R, FS[1]), BF),
            vmem((BR, FS[0]), BF),
            vmem((FS[0], BR), BF),
            vmem((2, OWN, FS[0]), BF),
            vmem((2, OWN, FS[1]), BF),
        ),
        in_specs=[hbm] * 10,
        out_specs=(in_vmem,) * 5,
        scratch_shapes=[
            vmem((TOK, D), BF),
            vmem((NZ, NX, BR, RY), BF),
            vmem((2, BR, R), BF),
            vmem((TOK, RY), F32),
            vmem((2, NX * TOK, Q), BF),
            vmem((2, TOK, Q), BF),
            vmem((R, NX * TOK), BF),
            vmem((2, NZ, ZROWS, Q), F32),
            vmem((2, 2, 4, ZROWS, QS[0]), BF),
            vmem((2, 2, 4, ZROWS, QS[1]), BF),
            vmem((2, 2, 4, ZROWS, QS[0]), BF),
            vmem((2, 2, 4, ZROWS, QS[1]), BF),
            vmem((2, NX, OWN, QS[0]), BF),
            vmem((2, NX, OWN, QS[1]), BF),
            vmem((4, OWN, FD), F32),
            vmem((2, R, FS[0]), BF),
            pltpu.SemaphoreType.DMA((N_SEM,)),
            pltpu.SemaphoreType.DMA((N_SEM,)),
            pltpu.SemaphoreType.DMA((16,)),
        ],
        compiler_params=pltpu.CompilerParams(
            collective_id=0, has_side_effects=True, vmem_limit_bytes=40 * 1024 * 1024
        ),
    )(*(pltpu.with_memory_space_constraint(v, pltpu.HBM) for v in operands))
    small = jax.ShapeDtypeStruct((OWN, FD), F32)
    return pl.pallas_call(
        finish,
        out_shape=(
            jax.ShapeDtypeStruct((BR, FD), BF),
            jax.ShapeDtypeStruct((FD, BR), BF),
            small,
            small,
            small,
            small,
        ),
        in_specs=[in_vmem] * 11,
        out_specs=(hbm,) * 6,
        scratch_shapes=[
            vmem((BR, FS[1]), BF),
            vmem((FS[1], BR), BF),
            vmem((2, 2, OWN, FD), F32),
            pltpu.SemaphoreType.DMA((4 + 4 * NX,)),
        ],
        compiler_params=pltpu.CompilerParams(vmem_limit_bytes=16 * 1024 * 1024),
    )(*kept, basis_up, basis_down, *moments)


def solution(mesh):
    row, both = P("dp", None), P("dp", "tensor")
    return jax.shard_map(
        local,
        mesh=mesh,
        in_specs=(row, row, both, both, row, row, both, both, both, both),
        out_specs=(both, P("tensor", "dp"), both, both, both, both),
        check_vma=False,
    )
```

```python
import functools

import jax
import jax.numpy as jnp
from jax import lax
from jax.experimental import pallas as pl
from jax.experimental.pallas import tpu as pltpu
from jax.sharding import PartitionSpec as P

STEPS = 1000
momentum_decay = 0.9
square_decay = 0.999
adam_epsilon = 1e-08
update_scale = 2.5
first_fix = 1.0 - momentum_decay**STEPS
second_fix = 1.0 - square_decay**STEPS

MESH = pl.DeviceIdType.MESH
BF, F32 = jnp.bfloat16, jnp.float32

NX, NY, NZ = 4, 4, 8
TOK, D, R, FD = 128, 8192, 512, 3584
BR = D // (NX * NZ)
RY = R // NY
Q = FD // NX
OWN = R // (NX * NZ)
ZROWS = NX * OWN
QS, QO = (512, 384), (0, 512)
FS = tuple(NX * w for w in QS)
DEPTH = 2
W1 = (1408, 768)
TILE = 512
N_SEM = 320


def kernel(
    tokens,
    out_grad,
    up_grad,
    hidden,
    basis_up,
    basis_down,
    m_up,
    v_up,
    m_down,
    v_down,
    steps1,
    d_up,
    d_down,
    gr0,
    gr1,
    t_buf,
    b_all,
    b_own,
    acc,
    u_buf,
    relay,
    pt,
    g_buf,
    rs_out0,
    rs_out1,
    rs_in0,
    rs_in1,
    gx0,
    gx1,
    mom,
    steps0,
    ssem,
    rsem,
    lsem,
):
    dp, tn = lax.axis_index("dp"), lax.axis_index("tensor")
    x, z = lax.div(dp, NZ), lax.rem(dp, NZ)
    y, c = lax.div(tn, 2), lax.rem(tn, 2)

    def wrap(v, n):
        return lax.rem(v + n, n)

    def at(xo=0, zo=0, yo=0, co=0):
        return (
            wrap(x + xo, NX) * NZ + wrap(z + zo, NZ),
            wrap(y + yo, NY) * 2 + lax.rem(c + co, 2),
        )

    def x_dev(xx):
        return (xx * NZ + z, tn)

    used = [0]
    pending = []
    slow = []
    done = [0]
    marks = []

    def drain():
        marks.append(len(pending))
        for cp in pending[done[0] : marks[-DEPTH]] if len(marks) >= DEPTH else ():
            cp.wait_send()
            done[0] += 1

    def take(n):
        used[0] += n
        return used[0] - n

    def remote(src, dst, dev, k, rk):
        return pltpu.make_async_remote_copy(
            src_ref=src,
            dst_ref=dst,
            send_sem=ssem.at[k],
            recv_sem=rsem.at[rk],
            device_id=dev,
            device_id_type=MESH,
        )

    def send(src, dst, dev, k=None, rk=None, sent=pending):
        k = take(1) if k is None else k
        cp = remote(src, dst, dev, k, k if rk is None else rk)
        cp.start()
        sent.append(cp)
        return cp

    def landed(ref, rk):
        remote(ref, ref, at(co=1), 0, rk).wait_recv()

    local_used = [0]

    def load(src, dst):
        k = local_used[0]
        local_used[0] += 1
        cp = pltpu.make_async_copy(src, dst, lsem.at[k])
        cp.start()
        return cp

    def load_by_core(src0, src1, dst):
        k = local_used[0]
        local_used[0] += 1

        @pl.when(c == 0)
        def _():
            pltpu.make_async_copy(src0, dst, lsem.at[k]).start()

        @pl.when(c == 1)
        def _():
            pltpu.make_async_copy(src1, dst, lsem.at[k]).start()

        return pltpu.make_async_copy(src0, dst, lsem.at[k])

    def quarter(q):
        return pl.ds(pl.multiple_of(q * Q, 128), Q)

    def tok_rows(q):
        return pl.ds(pl.multiple_of(q * TOK, TOK), TOK)

    y_cols = pl.ds(pl.multiple_of(y * RY, RY), RY)

    b_reg0 = b_all.at[x, z]
    own_b = load_by_core(basis_up.at[:, y_cols], basis_down.at[:, y_cols], b_reg0)
    own_t = load_by_core(tokens, out_grad, t_buf)
    ins = (up_grad, hidden)
    own_u = load_by_core(
        up_grad.at[:, quarter(x)], hidden.at[:, quarter(x)], u_buf.at[c, tok_rows(x), :]
    )
    own_bases = [load(r, b_own.at[k]) for k, r in enumerate((basis_up, basis_down))]
    own_m = [load(r, mom.at[k]) for k, r in enumerate((m_up, v_up, m_down, v_down))]

    partners = [at(xo=i, yo=j) for i in range(NX) for j in range(NY) if i or j]
    partners += [at(xo=i, co=1) for i in range(NX)]
    partners += [at(zo=1), at(zo=-1)]
    barrier = pltpu.get_barrier_semaphore()
    for dev in partners:
        pl.semaphore_signal(barrier, inc=1, device_id=dev, device_id_type=MESH)
    acc[...] = jnp.zeros_like(acc)
    own_b.wait()
    pl.semaphore_wait(barrier, len(partners))

    dirs = (1, -1)

    def b_reg(xo, zo, half=None):
        ref = b_all.at[wrap(x + xo, NX), wrap(z + zo, NZ)]
        if half is None:
            return ref
        return ref.at[pl.ds(half * (BR // 2), BR // 2), :]

    def gather_xz(reg, direct):
        hx, hz = {}, {}

        def z_first(xb):
            for d in dirs:
                blk = reg(xb, 0)
                hz[xb, d, 1] = send(blk, blk, at(zo=d))

        def z_step(xb, k):
            for d in dirs:
                hz[xb, d, k].wait_recv()
                if k < 4:
                    half = None if k < 3 else (0 if d > 0 else 1)
                    blk = reg(xb, -d * k, half)
                    hz[xb, d, k + 1] = send(blk, blk, at(zo=d))
            return [(xb, k), (xb, -k)] if k < 4 else [(xb, 4)]

        def r0():
            blk = reg(0, 0)
            for d in dirs:
                hx[d, 1] = send(blk, blk, at(xo=d))
            if direct:
                hx[2] = send(blk, blk, at(xo=2))
            z_first(0)
            return [(0, 0)]

        def r1():
            for d in dirs:
                hx[d, 1].wait_recv()
                if not direct:
                    blk = reg(-d, 0, 0 if d > 0 else 1)
                    hx[d, 2] = send(blk, blk, at(xo=d))
            z_first(-1)
            z_first(1)
            return [(-1, 0), (1, 0)]

        def r2():
            done = z_step(0, 1)
            if direct:
                hx[2].wait_recv()
            else:
                for d in dirs:
                    hx[d, 2].wait_recv()
            z_first(2)
            return done + [(2, 0)]

        def later(pairs):
            def run():
                done = []
                for xb, k in pairs:
                    done += z_step(xb, k)
                return done

            return run

        if direct:
            return [
                r0,
                r1,
                r2,
                later([(-1, 1), (1, 1), (2, 1), (0, 2)]),
                later([(-1, 2), (1, 2), (2, 2), (0, 3)]),
                later([(-1, 3), (1, 3), (2, 3), (0, 4)]),
                later([(-1, 4), (1, 4), (2, 4)]),
            ]
        return [
            r0,
            r1,
            r2,
            later([(0, 2), (-1, 1), (1, 1)]),
            later([(0, 3), (-1, 2), (1, 2), (2, 1)]),
            later([(0, 4), (-1, 3), (1, 3), (2, 2)]),
            later([(-1, 4), (1, 4), (2, 3)]),
            later([(2, 4)]),
        ]

    def project(blocks):
        for xo, zo in blocks:
            xx, zz = wrap(x + xo, NX), wrap(z + zo, NZ)
            cols = pl.ds(pl.multiple_of((xx * NZ + zz) * BR, BR), BR)
            acc[...] += jnp.dot(t_buf[:, cols], b_all[xx, zz], preferred_element_type=F32)

    x1 = x + 1 - 2 * lax.rem(x, 2)
    x3 = NX - 1 - x
    x2 = lax.rem(x + 2, NX)
    near = ((x1, x3), (x3, x1))
    my_p1 = x1 + c * (x3 - x1)
    my_p2 = x3 + c * (x1 - x3)

    def core_dev(xx, m):
        return (xx * NZ + z, y * 2 + m)

    rounds = gather_xz(b_reg, True)
    blocks = rounds[0]()
    got_b, got_a, got_c = take(2), take(2), take(2)
    for m in (0, 1):
        p1, p2 = near[m]
        send(ins[m].at[:, quarter(x2)], relay.at[c], core_dev(p1, m), rk=got_b + c, sent=slow)
    for m in (0, 1):
        p1, p2 = near[m]
        send(ins[m].at[:, quarter(p1)], u_buf.at[c, tok_rows(x), :], core_dev(p1, m), rk=got_a + c, sent=slow)
    for m in (0, 1):
        p1, p2 = near[m]
        send(ins[m].at[:, quarter(p2)], u_buf.at[c, tok_rows(x), :], core_dev(p2, m), rk=got_c + c, sent=slow)
    k_own = take(1)
    own_there = [
        remote(ins[m].at[:, quarter(x)], u_buf.at[c, tok_rows(x), :], at(co=1), k_own, k_own)
        for m in (0, 1)
    ]

    @pl.when(c == 1)
    def _():
        own_there[0].start()

    @pl.when(c == 0)
    def _():
        own_there[1].start()

    slow.append(own_there[0])
    hd = []
    own_t.wait()
    project(blocks)
    for k in range(1, len(rounds)):
        blocks = rounds[k]()
        if k == 3:
            for h in (0, 1):
                landed(relay.at[h], got_b + h)
                hd.append(send(relay.at[h], u_buf.at[h, tok_rows(my_p1), :], x_dev(my_p2), sent=slow))
        project(blocks)
        drain()

    mine = pt.at[y_cols, tok_rows(x)]
    mine[...] = acc[...].T.astype(BF)
    hp = {}
    for xo in (2, 1, -1, 0):
        for yo in range(NY):
            if xo == 0 and yo == 0:
                continue
            hp[xo, yo] = send(mine, mine, at(xo=xo, yo=yo))
    own_u.wait()
    landed(u_buf.at[1 - c, tok_rows(x), :], k_own)
    for h in (0, 1):
        landed(u_buf.at[h, tok_rows(my_p1), :], got_a + h)
        landed(u_buf.at[h, tok_rows(my_p2), :], got_c + h)
    for cp in hd:
        cp.wait_recv()
    for key, cp in hp.items():
        cp.wait_recv()

    def cols_of(st):
        return pl.ds(QO[st], QS[st])

    def gradient(st, h):
        for k in range(NX):
            rows = pt[k * NZ * OWN : (k + 1) * NZ * OWN, :]
            part = jnp.dot(rows, u_buf[h, :, cols_of(st)], preferred_element_type=F32)
            g_buf[h, :, k * OWN : (k + 1) * OWN, cols_of(st)] = part.reshape(NZ, OWN, QS[st])

    rs_out, rs_in, gx, gr, steps = (rs_out0, rs_out1), (rs_in0, rs_in1), (gx0, gx1), (gr0, gr1), (steps0, steps1)
    hr = {}
    reach = {(0, 1): 3, (0, -1): 4, (1, 1): 4, (1, -1): 3}

    def rs_step(st, h, s):
        for j, d in enumerate(dirs):
            n = reach[h, d]
            if s >= n:
                continue
            val = g_buf[h, wrap(z + d * (n - s), NZ), :, cols_of(st)]
            if s:
                hr[st, h, d, s - 1].wait_recv()
                val = val + rs_in[st][h, j, s - 1].astype(F32)
            rs_out[st][h, j, s] = val.astype(BF)
            hr[st, h, d, s] = send(rs_out[st].at[h, j, s], rs_in[st].at[h, j, s], at(zo=d))

    got_g = [[take(2) for _ in range(1, NX)] for st in (0, 1)]
    k_g = [take(1) for st in (0, 1)]

    def place(st, q):
        return pl.ds(pl.multiple_of(q * QS[st], 128), QS[st])

    def to_owners(st):
        for h in (0, 1):
            val = g_buf[h, z, :, cols_of(st)]
            for j, d in enumerate(dirs):
                n = reach[h, d]
                hr[st, h, d, n - 1].wait_recv()
                val = val + rs_in[st][h, j, n - 1].astype(F32)
            gx[st][h] = val.astype(BF).reshape(NX, OWN, QS[st])
            for k in range(1, NX):
                xx = wrap(x + k, NX)
                dst = gr[st].at[c, :, place(st, x)]
                send(gx[st].at[h, xx], dst, core_dev(xx, h), rk=got_g[st][k - 1] + c)
        gr[st][c, :, place(st, x)] = gx[st][c, x]
        send(gx[st].at[1 - c, x], gr[st].at[c, :, place(st, x)], at(co=1), k=k_g[st])

    own_rows = pl.ds(pl.multiple_of(dp * OWN, OWN), OWN)

    def adam(st):
        landed(gr[st].at[1 - c, :, place(st, x)], k_g[st])
        for m in (0, 1):
            for k in range(1, NX):
                landed(gr[st].at[m, :, place(st, wrap(x - k, NX))], got_g[st][k - 1] + m)
            for q in range(NX):
                cols = pl.ds(q * Q + QO[st], QS[st])
                here = pl.ds(q * QS[st], QS[st])
                grad = gr[st][m, :, here].astype(F32)
                moment = momentum_decay * mom[2 * m, :, cols] + (1.0 - momentum_decay) * grad
                second = square_decay * mom[2 * m + 1, :, cols] + (1.0 - square_decay) * grad * grad
                step = (
                    update_scale
                    * (moment * (1.0 / first_fix))
                    / (jnp.sqrt(second * (1.0 / second_fix)) + adam_epsilon)
                )
                steps[st][m, own_rows, here] = step.astype(BF)

    def gather_zx(reg):
        hz, hx = {}, {}

        def x_first(zo):
            for d in dirs:
                blk = reg(0, zo)
                hx[zo, d, 1] = send(blk, blk, at(xo=d))

        def x_relay(zo):
            for d in dirs:
                hx[zo, d, 1].wait_recv()
                blk = reg(-d, zo, 0 if d > 0 else 1)
                hx[zo, d, 2] = send(blk, blk, at(xo=d))

        def z_step(k):
            for d in dirs:
                hz[d, k].wait_recv()
                if k < 4:
                    blk = reg(0, -d * k, None if k < 3 else (0 if d > 0 else 1))
                    hz[d, k + 1] = send(blk, blk, at(zo=d))
            if k < 4:
                x_first(-k)
                x_first(k)
            else:
                x_first(4)

        def r0():
            for d in dirs:
                blk = reg(0, 0)
                hz[d, 1] = send(blk, blk, at(zo=d))
            x_first(0)

        def r1():
            z_step(1)
            x_relay(0)

        def r2():
            z_step(2)
            x_relay(-1)
            x_relay(1)

        def r3():
            z_step(3)

        def r4():
            z_step(4)
            x_relay(-2)
            x_relay(2)

        def r5():
            x_relay(-3)
            x_relay(3)

        def r6():
            x_relay(4)

        def r7():
            for zo in (0, -1, 1, -2, 2, -3, 3, 4):
                for d in dirs:
                    hx[zo, d, 2].wait_recv()

        return [r0, r1, r2, r3, r4, r5, r6, r7]

    def s_reg(st, lo, hi):
        def reg(xo, zo, half=None):
            rows = (wrap(x + xo, NX) * NZ + wrap(z + zo, NZ)) * OWN
            rows = pl.ds(pl.multiple_of(rows, OWN), OWN)
            return steps[st].at[slice(None) if half is None else half, rows, lo:hi]

        return reg

    plans = [
        (gather_xz(s_reg(st, W1[st], FS[st]), False), gather_zx(s_reg(st, 0, W1[st])))
        for st in (0, 1)
    ]

    def run_round(st, k):
        for plan in plans[st]:
            plan[k]()

    def update():
        for t in range(FS[0] // TILE):
            cols = pl.ds(t * TILE, TILE)
            val = jnp.dot(b_own[0], steps0[0, :, cols], preferred_element_type=F32)
            d_up[:, cols] = val.astype(BF)
            val = jnp.dot(b_own[1], steps0[1, :, cols], preferred_element_type=F32)
            d_down[cols, :] = val.T.astype(BF)

    for st in (0, 1):
        for h in (0, 1):
            gradient(st, h)
            rs_step(st, h, 0)
    for cp in slow:
        cp.wait_send()
    for k in range(1, 4):
        drain()
        for st in (0, 1):
            for h in (0, 1):
                rs_step(st, h, k)
    to_owners(0)
    to_owners(1)
    for cp in own_m + own_bases:
        cp.wait()
    adam(0)
    run_round(0, 0)
    adam(1)
    run_round(1, 0)
    for k in range(1, 7):
        run_round(0, k)
        run_round(1, k)
        drain()
    run_round(0, 7)
    update()
    run_round(1, 7)
    for cp in pending[done[0] :]:
        cp.wait_send()
    assert used[0] <= N_SEM, used[0]


def finish(
    steps1,
    d_up0,
    d_down0,
    gr0,
    gr1,
    basis_up,
    basis_down,
    m_up,
    v_up,
    m_down,
    v_down,
    delta_up,
    delta_down,
    next_m_up,
    next_v_up,
    next_m_down,
    next_v_down,
    d_up,
    d_down,
    new,
    sem,
):
    cps = []

    def store(src, dst):
        cp = pltpu.make_async_copy(src, dst, sem.at[len(cps)])
        cp.start()
        cps.append(cp)

    def places(st, q):
        return pl.ds(q * QS[st], QS[st]), pl.ds(q * Q + QO[st], QS[st])

    for q in range(NX):
        here, there = places(0, q)
        store(d_up0.at[:, here], delta_up.at[:, there])
        store(d_down0.at[here, :], delta_down.at[there, :])
    old = ((m_up, v_up), (m_down, v_down))
    outs = ((next_m_up, next_v_up), (next_m_down, next_v_down))
    for k in (0, 1):
        for st, gr in enumerate((gr0, gr1)):
            for q in range(NX):
                here, there = places(st, q)
                grad = gr[k, :, here].astype(F32)
                moment, second = old[k][0][:, there], old[k][1][:, there]
                new[k, 0, :, there] = momentum_decay * moment + (1.0 - momentum_decay) * grad
                new[k, 1, :, there] = square_decay * second + (1.0 - square_decay) * grad * grad
        for j in (0, 1):
            store(new.at[k, j], outs[k][j])
    for q in range(NX):
        here, there = places(1, q)
        val = jnp.dot(basis_down[...], steps1[1, :, here], preferred_element_type=F32)
        d_down[here, :] = val.T.astype(BF)
        store(d_down.at[here, :], delta_down.at[there, :])
        val = jnp.dot(basis_up[...], steps1[0, :, here], preferred_element_type=F32)
        d_up[:, here] = val.astype(BF)
        store(d_up.at[:, here], delta_up.at[:, there])
    for cp in cps:
        cp.wait()


def local(
    tokens_in,
    out_grad,
    up_grad,
    hidden_act,
    basis_up,
    basis_down,
    moment_up,
    second_up,
    moment_down,
    second_down,
):
    hbm = pl.BlockSpec(memory_space=pl.ANY)
    in_vmem = pl.BlockSpec(memory_space=pltpu.VMEM)
    vmem = pltpu.VMEM
    moments = (moment_up, second_up, moment_down, second_down)
    operands = (tokens_in, out_grad, up_grad, hidden_act, basis_up, basis_down, *moments)
    kept = pl.pallas_call(
        kernel,
        out_shape=(
            vmem((2, R, FS[1]), BF),
            vmem((BR, FS[0]), BF),
            vmem((FS[0], BR), BF),
            vmem((2, OWN, FS[0]), BF),
            vmem((2, OWN, FS[1]), BF),
        ),
        in_specs=[hbm] * 10,
        out_specs=(in_vmem,) * 5,
        scratch_shapes=[
            vmem((TOK, D), BF),
            vmem((NX, NZ, BR, RY), BF),
            vmem((2, BR, R), BF),
            vmem((TOK, RY), F32),
            vmem((2, NX * TOK, Q), BF),
            vmem((2, TOK, Q), BF),
            vmem((R, NX * TOK), BF),
            vmem((2, NZ, ZROWS, Q), F32),
            vmem((2, 2, 4, ZROWS, QS[0]), BF),
            vmem((2, 2, 4, ZROWS, QS[1]), BF),
            vmem((2, 2, 4, ZROWS, QS[0]), BF),
            vmem((2, 2, 4, ZROWS, QS[1]), BF),
            vmem((2, NX, OWN, QS[0]), BF),
            vmem((2, NX, OWN, QS[1]), BF),
            vmem((4, OWN, FD), F32),
            vmem((2, R, FS[0]), BF),
            pltpu.SemaphoreType.DMA((N_SEM,)),
            pltpu.SemaphoreType.DMA((N_SEM,)),
            pltpu.SemaphoreType.DMA((16,)),
        ],
        compiler_params=pltpu.CompilerParams(
            collective_id=0, has_side_effects=True, vmem_limit_bytes=40 * 1024 * 1024
        ),
    )(*(pltpu.with_memory_space_constraint(v, pltpu.HBM) for v in operands))
    small = jax.ShapeDtypeStruct((OWN, FD), F32)
    return pl.pallas_call(
        finish,
        out_shape=(
            jax.ShapeDtypeStruct((BR, FD), BF),
            jax.ShapeDtypeStruct((FD, BR), BF),
            small,
            small,
            small,
            small,
        ),
        in_specs=[in_vmem] * 11,
        out_specs=(hbm,) * 6,
        scratch_shapes=[
            vmem((BR, FS[1]), BF),
            vmem((FS[1], BR), BF),
            vmem((2, 2, OWN, FD), F32),
            pltpu.SemaphoreType.DMA((4 + 4 * NX,)),
        ],
        compiler_params=pltpu.CompilerParams(vmem_limit_bytes=16 * 1024 * 1024),
    )(*kept, basis_up, basis_down, *moments)


def solution(mesh):
    row, both = P("dp", None), P("dp", "tensor")
    return jax.shard_map(
        local,
        mesh=mesh,
        in_specs=(row, row, both, both, row, row, both, both, both, both),
        out_specs=(both, P("tensor", "dp"), both, both, both, both),
        check_vma=False,
    )
```

```python
import functools

import jax
import jax.numpy as jnp
from jax import lax
from jax.experimental import pallas as pl
from jax.experimental.pallas import tpu as pltpu
from jax.sharding import PartitionSpec as P

STEPS = 1000
momentum_decay = 0.9
square_decay = 0.999
adam_epsilon = 1e-08
update_scale = 2.5
first_fix = 1.0 - momentum_decay**STEPS
second_fix = 1.0 - square_decay**STEPS

MESH = pl.DeviceIdType.MESH
BF, F32 = jnp.bfloat16, jnp.float32

NX, NY, NZ = 4, 4, 8
TOK, D, R, FD = 128, 8192, 512, 3584
BR = D // (NX * NZ)
RY = R // NY
Q = FD // NX
OWN = R // (NX * NZ)
ZROWS = NX * OWN
QS, QO = (512, 384), (0, 512)
FS = tuple(NX * w for w in QS)
DEPTH = 2
W1 = (1408, 768)
TILE = 512
N_SEM = 320


def kernel(
    tokens,
    out_grad,
    up_grad,
    hidden,
    basis_up,
    basis_down,
    m_up,
    v_up,
    m_down,
    v_down,
    steps1,
    d_up,
    d_down,
    new,
    gr0,
    gr1,
    t_buf,
    b_all,
    b_own,
    acc,
    u_buf,
    relay,
    pt,
    g_buf,
    rs_out0,
    rs_out1,
    rs_in0,
    rs_in1,
    gx0,
    gx1,
    mom,
    steps0,
    ssem,
    rsem,
    lsem,
):
    dp, tn = lax.axis_index("dp"), lax.axis_index("tensor")
    x, z = lax.div(dp, NZ), lax.rem(dp, NZ)
    y, c = lax.div(tn, 2), lax.rem(tn, 2)

    def wrap(v, n):
        return lax.rem(v + n, n)

    def at(xo=0, zo=0, yo=0, co=0):
        return (
            wrap(x + xo, NX) * NZ + wrap(z + zo, NZ),
            wrap(y + yo, NY) * 2 + lax.rem(c + co, 2),
        )

    def x_dev(xx):
        return (xx * NZ + z, tn)

    used = [0]
    pending = []
    slow = []
    done = [0]
    marks = []

    def drain():
        marks.append(len(pending))
        for cp in pending[done[0] : marks[-DEPTH]] if len(marks) >= DEPTH else ():
            cp.wait_send()
            done[0] += 1

    def take(n):
        used[0] += n
        return used[0] - n

    def remote(src, dst, dev, k, rk):
        return pltpu.make_async_remote_copy(
            src_ref=src,
            dst_ref=dst,
            send_sem=ssem.at[k],
            recv_sem=rsem.at[rk],
            device_id=dev,
            device_id_type=MESH,
        )

    def send(src, dst, dev, k=None, rk=None, sent=pending):
        k = take(1) if k is None else k
        cp = remote(src, dst, dev, k, k if rk is None else rk)
        cp.start()
        sent.append(cp)
        return cp

    def landed(ref, rk):
        remote(ref, ref, at(co=1), 0, rk).wait_recv()

    local_used = [0]

    def load(src, dst):
        k = local_used[0]
        local_used[0] += 1
        cp = pltpu.make_async_copy(src, dst, lsem.at[k])
        cp.start()
        return cp

    def load_by_core(src0, src1, dst):
        k = local_used[0]
        local_used[0] += 1

        @pl.when(c == 0)
        def _():
            pltpu.make_async_copy(src0, dst, lsem.at[k]).start()

        @pl.when(c == 1)
        def _():
            pltpu.make_async_copy(src1, dst, lsem.at[k]).start()

        return pltpu.make_async_copy(src0, dst, lsem.at[k])

    def quarter(q):
        return pl.ds(pl.multiple_of(q * Q, 128), Q)

    def tok_rows(q):
        return pl.ds(pl.multiple_of(q * TOK, TOK), TOK)

    y_cols = pl.ds(pl.multiple_of(y * RY, RY), RY)

    b_reg0 = b_all.at[x, z]
    own_b = load_by_core(basis_up.at[:, y_cols], basis_down.at[:, y_cols], b_reg0)
    own_t = load_by_core(tokens, out_grad, t_buf)
    ins = (up_grad, hidden)
    own_u = load_by_core(
        up_grad.at[:, quarter(x)], hidden.at[:, quarter(x)], u_buf.at[c, tok_rows(x), :]
    )
    own_bases = [load(r, b_own.at[k]) for k, r in enumerate((basis_up, basis_down))]
    own_m = [load(r, mom.at[k]) for k, r in enumerate((m_up, v_up, m_down, v_down))]

    partners = [at(xo=i, yo=j) for i in range(NX) for j in range(NY) if i or j]
    partners += [at(xo=i, co=1) for i in range(NX)]
    partners += [at(zo=1), at(zo=-1)]
    barrier = pltpu.get_barrier_semaphore()
    for dev in partners:
        pl.semaphore_signal(barrier, inc=1, device_id=dev, device_id_type=MESH)
    acc[...] = jnp.zeros_like(acc)
    own_b.wait()
    pl.semaphore_wait(barrier, len(partners))

    dirs = (1, -1)

    def b_reg(xo, zo, half=None):
        ref = b_all.at[wrap(x + xo, NX), wrap(z + zo, NZ)]
        if half is None:
            return ref
        return ref.at[pl.ds(half * (BR // 2), BR // 2), :]

    def gather_xz(reg, direct):
        hx, hz = {}, {}

        def z_first(xb):
            for d in dirs:
                blk = reg(xb, 0)
                hz[xb, d, 1] = send(blk, blk, at(zo=d))

        def z_step(xb, k):
            for d in dirs:
                hz[xb, d, k].wait_recv()
                if k < 4:
                    half = None if k < 3 else (0 if d > 0 else 1)
                    blk = reg(xb, -d * k, half)
                    hz[xb, d, k + 1] = send(blk, blk, at(zo=d))
            return [(xb, k), (xb, -k)] if k < 4 else [(xb, 4)]

        def r0():
            blk = reg(0, 0)
            for d in dirs:
                hx[d, 1] = send(blk, blk, at(xo=d))
            if direct:
                hx[2] = send(blk, blk, at(xo=2))
            z_first(0)
            return [(0, 0)]

        def r1():
            for d in dirs:
                hx[d, 1].wait_recv()
                if not direct:
                    blk = reg(-d, 0, 0 if d > 0 else 1)
                    hx[d, 2] = send(blk, blk, at(xo=d))
            z_first(-1)
            z_first(1)
            return [(-1, 0), (1, 0)]

        def r2():
            done = z_step(0, 1)
            if direct:
                hx[2].wait_recv()
            else:
                for d in dirs:
                    hx[d, 2].wait_recv()
            z_first(2)
            return done + [(2, 0)]

        def later(pairs):
            def run():
                done = []
                for xb, k in pairs:
                    done += z_step(xb, k)
                return done

            return run

        if direct:
            return [
                r0,
                r1,
                r2,
                later([(-1, 1), (1, 1), (2, 1), (0, 2)]),
                later([(-1, 2), (1, 2), (2, 2), (0, 3)]),
                later([(-1, 3), (1, 3), (2, 3), (0, 4)]),
                later([(-1, 4), (1, 4), (2, 4)]),
            ]
        return [
            r0,
            r1,
            r2,
            later([(0, 2), (-1, 1), (1, 1)]),
            later([(0, 3), (-1, 2), (1, 2), (2, 1)]),
            later([(0, 4), (-1, 3), (1, 3), (2, 2)]),
            later([(-1, 4), (1, 4), (2, 3)]),
            later([(2, 4)]),
        ]

    def project(blocks):
        for xo, zo in blocks:
            xx, zz = wrap(x + xo, NX), wrap(z + zo, NZ)
            cols = pl.ds(pl.multiple_of((xx * NZ + zz) * BR, BR), BR)
            acc[...] += jnp.dot(t_buf[:, cols], b_all[xx, zz], preferred_element_type=F32)

    x1 = x + 1 - 2 * lax.rem(x, 2)
    x3 = NX - 1 - x
    x2 = lax.rem(x + 2, NX)
    near = ((x1, x3), (x3, x1))
    my_p1 = x1 + c * (x3 - x1)
    my_p2 = x3 + c * (x1 - x3)

    def core_dev(xx, m):
        return (xx * NZ + z, y * 2 + m)

    rounds = gather_xz(b_reg, True)
    blocks = rounds[0]()
    got_b, got_a, got_c = take(2), take(2), take(2)
    for m in (0, 1):
        p1, p2 = near[m]
        send(ins[m].at[:, quarter(x2)], relay.at[c], core_dev(p1, m), rk=got_b + c, sent=slow)
    for m in (0, 1):
        p1, p2 = near[m]
        send(ins[m].at[:, quarter(p1)], u_buf.at[c, tok_rows(x), :], core_dev(p1, m), rk=got_a + c, sent=slow)
    for m in (0, 1):
        p1, p2 = near[m]
        send(ins[m].at[:, quarter(p2)], u_buf.at[c, tok_rows(x), :], core_dev(p2, m), rk=got_c + c, sent=slow)
    k_own = take(1)
    own_there = [
        remote(ins[m].at[:, quarter(x)], u_buf.at[c, tok_rows(x), :], at(co=1), k_own, k_own)
        for m in (0, 1)
    ]

    @pl.when(c == 1)
    def _():
        own_there[0].start()

    @pl.when(c == 0)
    def _():
        own_there[1].start()

    slow.append(own_there[0])
    hd = []
    own_t.wait()
    project(blocks)
    for k in range(1, len(rounds)):
        blocks = rounds[k]()
        if k == 3:
            for h in (0, 1):
                landed(relay.at[h], got_b + h)
                hd.append(send(relay.at[h], u_buf.at[h, tok_rows(my_p1), :], x_dev(my_p2), sent=slow))
        project(blocks)
        drain()

    mine = pt.at[y_cols, tok_rows(x)]
    mine[...] = acc[...].T.astype(BF)
    hp = {}
    for xo in (2, 1, -1, 0):
        for yo in range(NY):
            if xo == 0 and yo == 0:
                continue
            hp[xo, yo] = send(mine, mine, at(xo=xo, yo=yo))
    own_u.wait()
    landed(u_buf.at[1 - c, tok_rows(x), :], k_own)
    for h in (0, 1):
        landed(u_buf.at[h, tok_rows(my_p1), :], got_a + h)
        landed(u_buf.at[h, tok_rows(my_p2), :], got_c + h)
    for cp in hd:
        cp.wait_recv()
    for key, cp in hp.items():
        cp.wait_recv()

    def cols_of(st):
        return pl.ds(QO[st], QS[st])

    def gradient(st, h):
        for k in range(NX):
            rows = pt[k * NZ * OWN : (k + 1) * NZ * OWN, :]
            part = jnp.dot(rows, u_buf[h, :, cols_of(st)], preferred_element_type=F32)
            g_buf[h, :, k * OWN : (k + 1) * OWN, cols_of(st)] = part.reshape(NZ, OWN, QS[st])

    rs_out, rs_in, gx, gr, steps = (rs_out0, rs_out1), (rs_in0, rs_in1), (gx0, gx1), (gr0, gr1), (steps0, steps1)
    hr = {}
    reach = {(0, 1): 3, (0, -1): 4, (1, 1): 4, (1, -1): 3}

    def rs_step(st, h, s):
        for j, d in enumerate(dirs):
            n = reach[h, d]
            if s >= n:
                continue
            val = g_buf[h, wrap(z + d * (n - s), NZ), :, cols_of(st)]
            if s:
                hr[st, h, d, s - 1].wait_recv()
                val = val + rs_in[st][h, j, s - 1].astype(F32)
            rs_out[st][h, j, s] = val.astype(BF)
            hr[st, h, d, s] = send(rs_out[st].at[h, j, s], rs_in[st].at[h, j, s], at(zo=d))

    got_g = [[take(2) for _ in range(1, NX)] for st in (0, 1)]
    k_g = [take(1) for st in (0, 1)]

    def place(st, q):
        return pl.ds(pl.multiple_of(q * QS[st], 128), QS[st])

    def to_owners(st):
        for h in (0, 1):
            val = g_buf[h, z, :, cols_of(st)]
            for j, d in enumerate(dirs):
                n = reach[h, d]
                hr[st, h, d, n - 1].wait_recv()
                val = val + rs_in[st][h, j, n - 1].astype(F32)
            gx[st][h] = val.astype(BF).reshape(NX, OWN, QS[st])
            for k in range(1, NX):
                xx = wrap(x + k, NX)
                dst = gr[st].at[c, :, place(st, x)]
                send(gx[st].at[h, xx], dst, core_dev(xx, h), rk=got_g[st][k - 1] + c)
        gr[st][c, :, place(st, x)] = gx[st][c, x]
        send(gx[st].at[1 - c, x], gr[st].at[c, :, place(st, x)], at(co=1), k=k_g[st])

    own_rows = pl.ds(pl.multiple_of(dp * OWN, OWN), OWN)

    def adam(st):
        landed(gr[st].at[1 - c, :, place(st, x)], k_g[st])
        for m in (0, 1):
            for k in range(1, NX):
                landed(gr[st].at[m, :, place(st, wrap(x - k, NX))], got_g[st][k - 1] + m)
            for q in range(NX):
                cols = pl.ds(q * Q + QO[st], QS[st])
                here = pl.ds(q * QS[st], QS[st])
                grad = gr[st][m, :, here].astype(F32)
                moment = momentum_decay * mom[2 * m, :, cols] + (1.0 - momentum_decay) * grad
                second = square_decay * mom[2 * m + 1, :, cols] + (1.0 - square_decay) * grad * grad
                new[2 * m, :, cols] = moment
                new[2 * m + 1, :, cols] = second
                step = (
                    update_scale
                    * (moment * (1.0 / first_fix))
                    / (jnp.sqrt(second * (1.0 / second_fix)) + adam_epsilon)
                )
                steps[st][m, own_rows, here] = step.astype(BF)

    def gather_zx(reg):
        hz, hx = {}, {}

        def x_first(zo):
            for d in dirs:
                blk = reg(0, zo)
                hx[zo, d, 1] = send(blk, blk, at(xo=d))

        def x_relay(zo):
            for d in dirs:
                hx[zo, d, 1].wait_recv()
                blk = reg(-d, zo, 0 if d > 0 else 1)
                hx[zo, d, 2] = send(blk, blk, at(xo=d))

        def z_step(k):
            for d in dirs:
                hz[d, k].wait_recv()
                if k < 4:
                    blk = reg(0, -d * k, None if k < 3 else (0 if d > 0 else 1))
                    hz[d, k + 1] = send(blk, blk, at(zo=d))
            if k < 4:
                x_first(-k)
                x_first(k)
            else:
                x_first(4)

        def r0():
            for d in dirs:
                blk = reg(0, 0)
                hz[d, 1] = send(blk, blk, at(zo=d))
            x_first(0)

        def r1():
            z_step(1)
            x_relay(0)

        def r2():
            z_step(2)
            x_relay(-1)
            x_relay(1)

        def r3():
            z_step(3)

        def r4():
            z_step(4)
            x_relay(-2)
            x_relay(2)

        def r5():
            x_relay(-3)
            x_relay(3)

        def r6():
            x_relay(4)

        def r7():
            for zo in (0, -1, 1, -2, 2, -3, 3, 4):
                for d in dirs:
                    hx[zo, d, 2].wait_recv()

        return [r0, r1, r2, r3, r4, r5, r6, r7]

    def s_reg(st, lo, hi):
        def reg(xo, zo, half=None):
            rows = (wrap(x + xo, NX) * NZ + wrap(z + zo, NZ)) * OWN
            rows = pl.ds(pl.multiple_of(rows, OWN), OWN)
            return steps[st].at[slice(None) if half is None else half, rows, lo:hi]

        return reg

    plans = [
        (gather_xz(s_reg(st, W1[st], FS[st]), False), gather_zx(s_reg(st, 0, W1[st])))
        for st in (0, 1)
    ]

    def run_round(st, k):
        for plan in plans[st]:
            plan[k]()

    def update():
        for t in range(FS[0] // TILE):
            cols = pl.ds(t * TILE, TILE)
            val = jnp.dot(b_own[0], steps0[0, :, cols], preferred_element_type=F32)
            d_up[:, cols] = val.astype(BF)
            val = jnp.dot(b_own[1], steps0[1, :, cols], preferred_element_type=F32)
            d_down[cols, :] = val.T.astype(BF)

    for st in (0, 1):
        for h in (0, 1):
            gradient(st, h)
            rs_step(st, h, 0)
    for cp in slow:
        cp.wait_send()
    for k in range(1, 4):
        drain()
        for st in (0, 1):
            for h in (0, 1):
                rs_step(st, h, k)
    to_owners(0)
    to_owners(1)
    for cp in own_m + own_bases:
        cp.wait()
    adam(0)
    run_round(0, 0)
    adam(1)
    run_round(1, 0)
    for k in range(1, 7):
        run_round(0, k)
        run_round(1, k)
        drain()
    run_round(0, 7)
    update()
    run_round(1, 7)
    for cp in pending[done[0] :]:
        cp.wait_send()
    assert used[0] <= N_SEM, used[0]


def finish(
    steps1,
    d_up0,
    d_down0,
    new,
    basis_up,
    basis_down,
    delta_up,
    delta_down,
    next_m_up,
    next_v_up,
    next_m_down,
    next_v_down,
    d_up,
    d_down,
    sem,
):
    cps = []

    def store(src, dst):
        cp = pltpu.make_async_copy(src, dst, sem.at[len(cps)])
        cp.start()
        cps.append(cp)

    def places(st, q):
        return pl.ds(q * QS[st], QS[st]), pl.ds(q * Q + QO[st], QS[st])

    for q in range(NX):
        here, there = places(0, q)
        store(d_up0.at[:, here], delta_up.at[:, there])
        store(d_down0.at[here, :], delta_down.at[there, :])
    for k, out in enumerate((next_m_up, next_v_up, next_m_down, next_v_down)):
        store(new.at[k], out)
    for q in range(NX):
        here, there = places(1, q)
        val = jnp.dot(basis_down[...], steps1[1, :, here], preferred_element_type=F32)
        d_down[here, :] = val.T.astype(BF)
        store(d_down.at[here, :], delta_down.at[there, :])
        val = jnp.dot(basis_up[...], steps1[0, :, here], preferred_element_type=F32)
        d_up[:, here] = val.astype(BF)
        store(d_up.at[:, here], delta_up.at[:, there])
    for cp in cps:
        cp.wait()


def local(
    tokens_in,
    out_grad,
    up_grad,
    hidden_act,
    basis_up,
    basis_down,
    moment_up,
    second_up,
    moment_down,
    second_down,
):
    hbm = pl.BlockSpec(memory_space=pl.ANY)
    in_vmem = pl.BlockSpec(memory_space=pltpu.VMEM)
    vmem = pltpu.VMEM
    moments = (moment_up, second_up, moment_down, second_down)
    operands = (tokens_in, out_grad, up_grad, hidden_act, basis_up, basis_down, *moments)
    kept = pl.pallas_call(
        kernel,
        out_shape=(
            vmem((2, R, FS[1]), BF),
            vmem((BR, FS[0]), BF),
            vmem((FS[0], BR), BF),
            vmem((4, OWN, FD), F32),
        ),
        in_specs=[hbm] * 10,
        out_specs=(in_vmem,) * 4,
        scratch_shapes=[
            vmem((2, OWN, FS[0]), BF),
            vmem((2, OWN, FS[1]), BF),
            vmem((TOK, D), BF),
            vmem((NX, NZ, BR, RY), BF),
            vmem((2, BR, R), BF),
            vmem((TOK, RY), F32),
            vmem((2, NX * TOK, Q), BF),
            vmem((2, TOK, Q), BF),
            vmem((R, NX * TOK), BF),
            vmem((2, NZ, ZROWS, Q), F32),
            vmem((2, 2, 4, ZROWS, QS[0]), BF),
            vmem((2, 2, 4, ZROWS, QS[1]), BF),
            vmem((2, 2, 4, ZROWS, QS[0]), BF),
            vmem((2, 2, 4, ZROWS, QS[1]), BF),
            vmem((2, NX, OWN, QS[0]), BF),
            vmem((2, NX, OWN, QS[1]), BF),
            vmem((4, OWN, FD), F32),
            vmem((2, R, FS[0]), BF),
            pltpu.SemaphoreType.DMA((N_SEM,)),
            pltpu.SemaphoreType.DMA((N_SEM,)),
            pltpu.SemaphoreType.DMA((16,)),
        ],
        compiler_params=pltpu.CompilerParams(
            collective_id=0, has_side_effects=True, vmem_limit_bytes=40 * 1024 * 1024
        ),
    )(*(pltpu.with_memory_space_constraint(v, pltpu.HBM) for v in operands))
    small = jax.ShapeDtypeStruct((OWN, FD), F32)
    return pl.pallas_call(
        finish,
        out_shape=(
            jax.ShapeDtypeStruct((BR, FD), BF),
            jax.ShapeDtypeStruct((FD, BR), BF),
            small,
            small,
            small,
            small,
        ),
        in_specs=[in_vmem] * 6,
        out_specs=(hbm,) * 6,
        scratch_shapes=[
            vmem((BR, FS[1]), BF),
            vmem((FS[1], BR), BF),
            pltpu.SemaphoreType.DMA((4 + 4 * NX,)),
        ],
        compiler_params=pltpu.CompilerParams(vmem_limit_bytes=16 * 1024 * 1024),
    )(*kept, basis_up, basis_down)


def solution(mesh):
    row, both = P("dp", None), P("dp", "tensor")
    return jax.shard_map(
        local,
        mesh=mesh,
        in_specs=(row, row, both, both, row, row, both, both, both, both),
        out_specs=(both, P("tensor", "dp"), both, both, both, both),
        check_vma=False,
    )
```
